128 devices in a mesh: dom: 16 (over z, x), sub: 8 (over y, core).
Axes of the slice: x: 4, y: 4, z: 4, core: 2. Of those that a mesh axis runs over, the one named last changes fastest.
Arguments:
- positions: float32 [3, 4194304], P(None, ('dom', 'sub')), may hold values from -0.11 to 1.11
- velocities: float32 [3, 4194304], P(None, ('dom', 'sub')), may hold values from -3 to 3
- masses: float32 [4194304], P(('dom', 'sub')), may hold values from 0.003 to 0.012
- accel_prev: float32 [3, 4194304], P(None, ('dom', 'sub')), may hold values from -180 to 180
- active: int32 [4194304], P(('dom', 'sub')), may hold values from 0 to 1, as said below
- bucket_top: int32 [16384], P(('dom', 'sub')), may hold values from 0 to 4095
- near_list: int32 [16384, 4], P(('dom', 'sub')), may hold values from 0 to 1023, as said below
- cell_list: int32 [16384, 64], P(('dom', 'sub')), may hold values from 0 to 4095
- top_list: int32 [16384, 32], P(('dom', 'sub')), may hold values from 0 to 4095
- essential: int32 [16, 8, 16, 32], P('dom', 'sub'), may hold values from 0 to 1023
- work: int32 [5120], P(('dom', 'sub')), may hold values from 0 to 1023, as said below
Outputs:
- vel_out: float32 [3, 4194304], P(None, ('dom', 'sub'))
- pos_out: float32 [3, 4194304], P(None, ('dom', 'sub'))
The draws below stay inside these ranges and needn't reach their ends.
Inputs may be any that keep to these rules, and one draw needn't show every extreme that they name: near_list[n, 0] is the group-local number of bucket n itself; every entry of row n names a bucket of n's group whose top cell differs from n's by at most one in each of the three top-cell coordinates. A bucket holds an active particle exactly when its group-local number appears in its group's block of work. `work`: entries g * 8 * 40 to (g + 1) * 8 * 40 - 1 are the block of domain group g and name distinct group-local buckets; in every group one device holds 128 of the named buckets.
All inputs are finite; a program needn't handle non-finite values.
Results may differ from the reference program's by a relative error of at most 0.0003.
Values sent between devices are 32-bit elements; how exact they have to be, the bound alone decides.
A program may use at most 64 MiB of HBM per device.

```python
import math
import jax
import jax.numpy as jnp
from jax import lax

BUCKET = 256
B_DEV = 128
W_DEV = 40
RS = 32
NB = 4
NC = 64
NT = 32
TOP_SIDE = 16
STEPS = 2
TOP = 4096
G_BUCK = 1024
NBUCK = 16384
NPART = 4194304
ESS = 4096
N_DOM = 16
N_SUB = 8


def activity_plan(base_key):
    group_keys = jax.random.split(base_key, N_DOM)

    def one_group(group_key):
        key_busy, key_select, key_shuffle = jax.random.split(group_key, 3)
        busiest = jax.random.randint(key_busy, (), 0, N_SUB)
        remaining = N_SUB * W_DEV - B_DEV
        selected = jax.random.permutation(key_select, (N_SUB - 1) * B_DEV)[:remaining].astype(jnp.int32)
        others = selected + B_DEV * (selected >= B_DEV * busiest).astype(jnp.int32)
        starred = busiest * B_DEV + jnp.arange(B_DEV, dtype=jnp.int32)
        chosen = jnp.concatenate([starred, others]).astype(jnp.int32)
        shuffled = jax.random.permutation(key_shuffle, chosen)
        bucket_marks = jnp.zeros((G_BUCK,), jnp.int32).at[chosen].set(1)
        return (shuffled.astype(jnp.int32), bucket_marks)
    return jax.vmap(one_group)(group_keys)


def draw_work(key, part):
    shuffled, bucket_marks = activity_plan(jax.random.fold_in(key, 11))
    return shuffled.reshape(-1).astype(jnp.int32)


def draw_active(key, part):
    shuffled, bucket_marks = activity_plan(jax.random.fold_in(key, 11))
    coin_flips = jax.random.randint(jax.random.fold_in(key, 12), (NBUCK, BUCKET), 0, 2)
    chosen_lane = jax.random.randint(jax.random.fold_in(key, 13), (NBUCK, 1), 0, BUCKET)
    lane_ids = jnp.arange(BUCKET, dtype=jnp.int32)[None, :]
    flags = jnp.maximum(coin_flips, (lane_ids == chosen_lane).astype(jnp.int32))
    flags = flags * bucket_marks.reshape(NBUCK, 1)
    return flags.reshape(-1).astype(jnp.int32)


def bucket_plan(base_key):
    cell_side = TOP_SIDE
    cluster_span = 4
    cluster_count = G_BUCK // cluster_span
    group_keys = jax.random.split(jax.random.fold_in(base_key, 21), N_DOM)
    starts = jax.random.randint(jax.random.fold_in(base_key, 24), (N_DOM, 3), 0, cell_side).astype(jnp.int32)
    starts = starts.at[0].set(0).at[N_DOM - 1].set(cell_side - 1)

    def one_group(group_key, start):
        key_order, key_moves, key_reach, key_sides = jax.random.split(group_key, 4)
        order = jax.random.permutation(key_order, G_BUCK).astype(jnp.int32)
        moves = jax.random.randint(key_moves, (3, cluster_count), -1, 2).astype(jnp.int32)
        moves = moves.at[:, 0].set(0)
        walk = jnp.clip(start[:, None] + jnp.cumsum(moves, axis=1), 0, cell_side - 1)
        cluster_top = (walk[0] * cell_side * cell_side + walk[1] * cell_side + walk[2]).astype(jnp.int32)
        slot_ids = jnp.arange(G_BUCK, dtype=jnp.int32)
        slot_top = cluster_top[slot_ids // cluster_span]
        reach = jax.random.randint(key_reach, (G_BUCK, NB - 1), 1, cluster_span + 1).astype(jnp.int32)
        sides = 2 * jax.random.randint(key_sides, (G_BUCK, NB - 1), 0, 2).astype(jnp.int32) - 1
        near_slots = jnp.clip(slot_ids[:, None] + reach * sides, 0, G_BUCK - 1)
        rows = jnp.concatenate([order[:, None], order[near_slots]], axis=1).astype(jnp.int32)
        tops = jnp.zeros((G_BUCK,), jnp.int32).at[order].set(slot_top)
        nearby = jnp.zeros((G_BUCK, NB), jnp.int32).at[order].set(rows)
        return (tops, nearby)
    tops, nearby = jax.vmap(one_group)(group_keys, starts)
    return (tops.reshape(NBUCK).astype(jnp.int32), nearby.reshape(NBUCK, NB).astype(jnp.int32))


def draw_bucket_top(key, part):
    tops, nearby = bucket_plan(key)
    return tops


def draw_near_list(key, part):
    tops, nearby = bucket_plan(key)
    return nearby


def draw_positions(key, part):
    top_ids, nearby = bucket_plan(key)
    cell_side = TOP_SIDE
    first_index = top_ids // (cell_side * cell_side)
    second_index = top_ids // cell_side % cell_side
    third_index = top_ids % cell_side
    centres = (jnp.stack([first_index, second_index, third_index]).astype(jnp.float32) + 0.5) / cell_side
    jitter = jax.random.uniform(jax.random.fold_in(key, 22), (3, NBUCK, 1), jnp.float32, -0.5, 0.5) / cell_side
    spread = 0.03 * jnp.clip(jax.random.normal(jax.random.fold_in(key, 23), (3, NBUCK, BUCKET), jnp.float32), -3.5, 3.5)
    places = centres[:, :, None] + jitter + spread
    return places.reshape(3, NPART).astype(jnp.float32)


def plant(values, own_key, low, high):
    spot = [jax.random.randint(jax.random.fold_in(own_key, axis), (), 0, length) for axis, length in enumerate(values.shape)]
    longest = values.shape.index(max(values.shape))
    beside = spot[:longest] + [(spot[longest] + 1) % values.shape[longest]] + spot[longest + 1:]
    return values.at[tuple(spot)].set(low).at[tuple(beside)].set(high)


def levels(key, extent, pieces, least, high):
    factor_of = 1.0
    for position, blocks in pieces:
        steps = jax.random.uniform(jax.random.fold_in(jax.random.fold_in(key, 6), position), (blocks,), jnp.float32, least / len(pieces), high / len(pieces))
        factor_of = factor_of * jnp.repeat(jnp.exp(steps), extent[position] // blocks).reshape((-1,) + (1,) * (len(extent) - 1 - position))
    return factor_of


def noise(key, shape, width, bound, cuts=(), kind=jnp.bfloat16):
    values = jax.random.normal(key, shape, jnp.float32) * width
    if len(cuts) > 0:
        values = levels(key, shape, cuts, -0.22, 0.18) * values
    return jnp.clip(values, min=-bound, max=bound).astype(kind)


def setup_inputs(seed: int = 0) -> dict:
    splits = jax.random.split(jax.random.key(seed), 12)
    positions = draw_positions(jax.random.fold_in(splits[11], 71), 0)
    velocities = noise(splits[1], (3, NPART), 0.5, 3.0, ((1, 128),), jnp.float32)
    masses = jnp.clip(jnp.exp(math.log(0.012) - 1.3862944 * jax.random.uniform(splits[2], (NPART,), jnp.float32) ** levels(splits[2], (NPART,), ((0, 128),), -0.2, 0.2)), 0.003, 0.012)
    accel_prev = noise(splits[3], (3, NPART), 30.0, 180.0, ((1, 128),), jnp.float32)
    active = draw_active(jax.random.fold_in(splits[11], 71), 0)
    bucket_top = draw_bucket_top(jax.random.fold_in(splits[11], 71), 0)
    near_list = draw_near_list(jax.random.fold_in(splits[11], 71), 0)
    cell_list = plant(jax.random.randint(splits[7], (NBUCK, NC), 0, ESS), jax.random.fold_in(splits[7], 1), 0, ESS - 1).astype(jnp.int32)
    top_list = plant(jax.random.randint(splits[8], (NBUCK, NT), 0, TOP), jax.random.fold_in(splits[8], 1), 0, TOP - 1).astype(jnp.int32)
    essential = plant(jax.random.randint(splits[9], (N_DOM, N_SUB, N_DOM, RS), 0, G_BUCK), jax.random.fold_in(splits[9], 1), 0, G_BUCK - 1).astype(jnp.int32)
    work = draw_work(jax.random.fold_in(splits[11], 71), 0)
    return dict(positions=positions, velocities=velocities, masses=masses, accel_prev=accel_prev, active=active, bucket_top=bucket_top, near_list=near_list, cell_list=cell_list, top_list=top_list, essential=essential, work=work)


time_step = 0.01
soften = 0.0025
mass_floor = 0.5

def top_centres(top_ids):
    cell_side = TOP_SIDE
    first_index = top_ids // (cell_side * cell_side)
    second_index = top_ids // cell_side % cell_side
    third_index = top_ids % cell_side
    stacked = jnp.stack([first_index, second_index, third_index]).astype(jnp.float32)
    return (stacked + 0.5) / cell_side

def bucket_moments(places, weights):
    mass_total = lax.optimization_barrier(jnp.sum(weights, axis=1))
    centre = lax.optimization_barrier(jnp.sum(places * weights[None], axis=2)) / mass_total[None]
    offsets = places - centre[:, :, None]
    radius_sq = lax.optimization_barrier(jnp.sum(offsets * offsets, axis=0))

    def diagonal(first_axis):
        return lax.optimization_barrier(jnp.sum(weights * (3.0 * offsets[first_axis] * offsets[first_axis] - radius_sq), axis=1))

    def crossed(first_axis, second_axis):
        return 3.0 * lax.optimization_barrier(jnp.sum(weights * offsets[first_axis] * offsets[second_axis], axis=1))
    quadrupole = jnp.stack([diagonal(0), diagonal(1), diagonal(2), crossed(0, 1), crossed(0, 2), crossed(1, 2)])
    return jnp.concatenate([mass_total[None], centre, quadrupole], axis=0)

def top_raw(places, weights, centres):
    offsets = places - centres[:, :, None]
    weighted = weights[None] * offsets
    row_list = [weights, weighted[0], weighted[1], weighted[2], weighted[0] * offsets[0], weighted[1] * offsets[1], weighted[2] * offsets[2], weighted[0] * offsets[1], weighted[0] * offsets[2], weighted[1] * offsets[2]]
    return jnp.stack([lax.optimization_barrier(jnp.sum(row_values, axis=1)) for row_values in row_list])

def top_moments(raw_sums, centres):
    mass_total = raw_sums[0]
    safe_mass = jnp.maximum(mass_total, mass_floor)
    first_sums = raw_sums[1:4]
    centre = centres + first_sums / safe_mass[None]
    cov_xx = raw_sums[4] - first_sums[0] * first_sums[0] / safe_mass
    cov_yy = raw_sums[5] - first_sums[1] * first_sums[1] / safe_mass
    cov_zz = raw_sums[6] - first_sums[2] * first_sums[2] / safe_mass
    cov_xy = raw_sums[7] - first_sums[0] * first_sums[1] / safe_mass
    cov_xz = raw_sums[8] - first_sums[0] * first_sums[2] / safe_mass
    cov_yz = raw_sums[9] - first_sums[1] * first_sums[2] / safe_mass
    trace_sum = cov_xx + cov_yy + cov_zz
    quadrupole = jnp.stack([3.0 * cov_xx - trace_sum, 3.0 * cov_yy - trace_sum, 3.0 * cov_zz - trace_sum, 3.0 * cov_xy, 3.0 * cov_xz, 3.0 * cov_yz])
    return jnp.concatenate([mass_total[None], centre, quadrupole], axis=0)

def pair_accel(targets, sources, source_mass):
    offsets = sources[:, :, None] - targets[:, None, :]
    distance = lax.optimization_barrier(jnp.sum(offsets * offsets, axis=0)) + soften
    inverse = lax.rsqrt(distance)
    strength = source_mass[:, None] * inverse * inverse * inverse
    return lax.optimization_barrier(jnp.sum(offsets * strength[None], axis=1))

def cell_accel(targets, moments):
    offsets = targets[:, None, :] - moments[1:4, :, None]
    distance = lax.optimization_barrier(jnp.sum(offsets * offsets, axis=0)) + soften
    inverse = lax.rsqrt(distance)
    inverse_sq = inverse * inverse
    inverse_three = inverse * inverse_sq
    inverse_five = inverse_three * inverse_sq
    inverse_seven = inverse_five * inverse_sq
    quadrupole = moments[4:10, :, None]
    along_x = quadrupole[0] * offsets[0] + quadrupole[3] * offsets[1] + quadrupole[4] * offsets[2]
    along_y = quadrupole[3] * offsets[0] + quadrupole[1] * offsets[1] + quadrupole[5] * offsets[2]
    along_z = quadrupole[4] * offsets[0] + quadrupole[5] * offsets[1] + quadrupole[2] * offsets[2]
    contracted = offsets[0] * along_x + offsets[1] * along_y + offsets[2] * along_z
    radial = -moments[0][:, None] * inverse_three - 2.5 * contracted * inverse_seven
    along_all = jnp.stack([along_x, along_y, along_z])
    return lax.optimization_barrier(jnp.sum(offsets * radial[None] + along_all * inverse_five[None], axis=1))

def force_one(target, near_ids, cell_ids, top_ids, group_places, group_mass, essential_cells, top_cells):
    sources = group_places[:, near_ids].reshape(3, -1)
    source_mass = group_mass[near_ids].reshape(-1)
    moments = jnp.concatenate([jnp.take(essential_cells, cell_ids, axis=1), jnp.take(top_cells, top_ids, axis=1)], axis=1)
    return pair_accel(target, sources, source_mass) + cell_accel(target, moments)

def in_blocks(step_function, inputs, item_count):
    block_width = 4 if item_count % 4 == 0 else 2 if item_count % 2 == 0 else 1

    def reshape_leaf(values):
        return values.reshape((item_count // block_width, block_width) + values.shape[1:])
    result = lax.map(jax.vmap(step_function), jax.tree.map(reshape_leaf, inputs))
    return result.reshape((item_count,) + result.shape[2:])

def reference(positions, velocities, masses, accel_prev, active, bucket_top, near_list, cell_list, top_list, essential, work):
    activity = active.astype(jnp.float32)
    group_offsets = jnp.arange(N_DOM, dtype=jnp.int32) * G_BUCK
    essential_ids = (essential + group_offsets[None, None, :, None]).reshape(N_DOM, ESS).astype(jnp.int32)
    work_groups = jnp.repeat(jnp.arange(N_DOM, dtype=jnp.int32), N_SUB * W_DEV)
    work_global = (work + work_groups * G_BUCK).astype(jnp.int32)
    bucket_centres = top_centres(bucket_top)
    cell_centres = top_centres(jnp.arange(TOP, dtype=jnp.int32))
    places = positions
    speeds = velocities
    accel_now = accel_prev
    for substep in range(STEPS):
        half_speed = speeds + 0.5 * time_step * activity * accel_now
        places = places + time_step * half_speed
        bucketed = places.reshape(3, NBUCK, BUCKET)
        bucket_mass = masses.reshape(NBUCK, BUCKET)
        bucket_cells = bucket_moments(bucketed, bucket_mass)
        per_bucket = top_raw(bucketed, bucket_mass, bucket_centres)
        summed = jax.ops.segment_sum(per_bucket.T, bucket_top, num_segments=TOP).T
        top_cells = top_moments(summed, cell_centres)

        def one_bucket(work_item):
            global_id, group_id = work_item
            near_ids = (near_list[global_id] + group_id * G_BUCK).astype(jnp.int32)
            cell_ids = essential_ids[group_id][cell_list[global_id]]
            return force_one(bucketed[:, global_id], near_ids, cell_ids, top_list[global_id], bucketed, bucket_mass, bucket_cells, top_cells)
        forces = in_blocks(one_bucket, (work_global, work_groups), N_DOM * N_SUB * W_DEV)
        spread_forces = jnp.zeros((3, NBUCK, BUCKET), jnp.float32).at[:, work_global].set(jnp.transpose(forces, (1, 0, 2)))
        accel_now = spread_forces.reshape(3, NPART)
        speeds = half_speed + 0.5 * time_step * activity * accel_now
    return (speeds, places)
```

```python
import jax
import jax.numpy as jnp
from jax import lax
from jax.experimental import pallas as pl
from jax.experimental.pallas import tpu as pltpu
from jax.sharding import PartitionSpec as P

f32, bf16, i32 = jnp.float32, jnp.bfloat16, jnp.int32
MESH = pl.DeviceIdType.MESH
SUB, DOM = 8, 16
BUCKETS, WIDE, ITEMS = 128, 256, 40
GROUP = SUB * BUCKETS
TOP_SIDE = 16
MIB = 2**20

time_step = 0.01
soften = 0.0025
mass_floor = 0.5
kick = 0.5 * time_step


def rnd(a):
    return a.astype(bf16).astype(f32)


def split3(a):
    h = rnd(a)
    r = a - h
    m = rnd(r)
    return h, m, rnd(r - m)


def dot(a, b, dims):
    return lax.dot_general(
        a.astype(bf16), b.astype(bf16), ((dims[:1], dims[1:]), ((), ())), preferred_element_type=f32
    )


def row_iota(shape):
    return lax.broadcasted_iota(i32, shape, 0)


def pick(rows, shape):
    at = row_iota(shape)
    out = jnp.zeros(shape, f32)
    for i, v in rows.items():
        out = jnp.where(at == i, v, out)
    return out


def square(y):
    q = y * y
    return q[0:1] + q[1:2] + q[2:3]


def moments(dense, top_row, rec_ref):
    first = [dense[c][:, 0:1] for c in range(3)]
    y = [dense[c] - first[c] for c in range(3)]
    m = dense[3]
    ones = jnp.ones((8, WIDE), f32)
    lead = jnp.where(lax.broadcasted_iota(i32, (8, WIDE), 1) == 0, 1.0, 0.0)

    def total(a, by=ones):
        return lax.dot_general(
            by, a, (((1,), (1,)), ((), ())), precision=lax.Precision.HIGHEST, preferred_element_type=f32
        )[0:1]

    my = [m * y[c] for c in range(3)]
    mass = total(m)
    start = [total(dense[c], lead) for c in range(3)]
    s = [total(my[c]) for c in range(3)]
    d = [s[c] / mass for c in range(3)]
    pairs = ((0, 0), (1, 1), (2, 2), (0, 1), (0, 2), (1, 2))
    second = [total(my[a] * y[b]) - s[a] * d[b] for a, b in pairs]
    rows = {0: mass, 10: top_row}
    for c in range(3):
        rows[1 + c] = start[c] + d[c]
    for k in range(6):
        rows[4 + k] = second[k]
    rec_ref[...] = pick(rows, (16, BUCKETS))


def first_kernel(pos, vel, acc, act, mass, top_row, half_ref, x4_ref, p4_ref, rec_ref, dense):
    def one(b, carry):
        sl = pl.ds(pl.multiple_of(b * WIDE, WIDE), WIDE)
        a = act[:, sl].astype(f32)
        h = vel[:, sl] + kick * a * acc[:, sl]
        x = pos[:, sl] + time_step * h
        half_ref[:, sl] = h
        m = mass[:, sl]
        x4_ref[b] = jnp.concatenate([x, m], axis=0)
        p4_ref[b] = jnp.concatenate([x + time_step * h, a], axis=0)
        for c in range(3):
            dense[c, pl.ds(b, 1), :] = x[c : c + 1]
        dense[3, pl.ds(b, 1), :] = m
        return carry

    lax.fori_loop(0, BUCKETS, one, 0, unroll=4)
    moments(dense, top_row[...], rec_ref)


def second_kernel(slot, x4, half, act, mass, top_row, force, half_ref, pos_ref, rec_ref, dense):
    def one(b, carry):
        sl = pl.ds(pl.multiple_of(b * WIDE, WIDE), WIDE)
        a = act[:, sl].astype(f32)
        f = jnp.where(slot[b] >= 0, force[jnp.maximum(slot[b], 0)][0:3], 0.0)
        push = kick * a * f
        h = half[:, sl] + push + push
        x = x4[b][0:3] + time_step * h
        half_ref[:, sl] = h
        pos_ref[:, sl] = x
        for c in range(3):
            dense[c, pl.ds(b, 1), :] = x[c : c + 1]
        dense[3, pl.ds(b, 1), :] = mass[:, sl]
        return carry

    lax.fori_loop(0, BUCKETS, one, 0, unroll=4)
    moments(dense, top_row[...], rec_ref)


def last_kernel(slot, half, act, force, vel_ref):
    def one(b, carry):
        sl = pl.ds(pl.multiple_of(b * WIDE, WIDE), WIDE)
        f = jnp.where(slot[b] >= 0, force[jnp.maximum(slot[b], 0)][0:3], 0.0)
        vel_ref[:, sl] = half[:, sl] + kick * act[:, sl].astype(f32) * f
        return carry

    lax.fori_loop(0, BUCKETS, one, 0, unroll=4)


def centre(ids):
    return [
        (part.astype(f32) + 0.5) / TOP_SIDE
        for part in (ids >> 8, (ids >> 4) & 15, ids & 15)
    ]


def cells_kernel(rec, out, top, part, sums, s1, r1, s2, r2, s3, r3, s4, r4):
    g, s = lax.axis_index("dom"), lax.axis_index("sub")
    across = [(lax.rem(g + k, DOM), s) for k in range(1, DOM)]
    within = [(g, lax.rem(s + k, SUB)) for k in range(1, SUB)]
    barrier = pltpu.get_barrier_semaphore()
    for peer in across + within:
        pl.semaphore_signal(barrier, inc=1, device_id=peer, device_id_type=MESH)
    pl.semaphore_wait(barrier, DOM + SUB - 2)

    def send(ref_from, ref_to, peers, sends, recvs):
        copies = [
            pltpu.make_async_remote_copy(
                src_ref=ref_from, dst_ref=ref_to, send_sem=sends.at[k], recv_sem=recvs.at[k],
                device_id=peer, device_id_type=MESH,
            )
            for k, peer in enumerate(peers)
        ]
        for c in copies:
            c.start()
        return copies

    def done(copies):
        for c in copies:
            c.wait()

    out[s, g] = rec[...]
    done(send(rec, out.at[s, g], across, s1, r1))
    done(send(out.at[s], out.at[s], within, s2, r2))

    base = (s * DOM + g) * 32
    ids = lax.broadcasted_iota(i32, (32, BUCKETS), 0) + base

    def values(t):
        mass = t[0:1]
        own = t[10:11].astype(i32)
        d = [t[1 + c : 2 + c] - at for c, at in enumerate(centre(own))]
        md = [mass * d[c] for c in range(3)]
        rows = {0: mass, 1: md[0], 2: md[1], 3: md[2]}
        for k, (a, b) in enumerate(((0, 0), (1, 1), (2, 2), (0, 1), (0, 2), (1, 2))):
            rows[4 + k] = t[4 + k : 5 + k] + md[a] * d[b]
        pieces = jnp.concatenate(split3(pick(rows, (16, BUCKETS))), axis=0)
        return pieces, jnp.where(ids == own, 1.0, 0.0)

    sums[...] = jnp.zeros_like(sums)

    def step(i, carry):
        row, k = i // 4, (i % 4) * 4
        got = [values(out[row, k + u]) for u in range(4)]
        v = jnp.concatenate([a for a, _ in got], axis=1)
        o = jnp.concatenate([b for _, b in got], axis=1)
        sums[...] += dot(v, o, (1, 1))
        return carry

    lax.fori_loop(0, SUB * DOM // 4, step, 0)
    t = sums[0:16] + sums[16:32] + sums[32:48]
    mass = t[0:1]
    w = jnp.maximum(mass, mass_floor)
    at = centre(lax.broadcasted_iota(i32, (1, 32), 1) + base)
    u = [t[1 + c : 2 + c] / w for c in range(3)]
    rows = {0: mass}
    for c in range(3):
        rows[1 + c] = at[c] + u[c]
    for k, (a, b) in enumerate(((0, 0), (1, 1), (2, 2), (0, 1), (0, 2), (1, 2))):
        rows[4 + k] = t[4 + k : 5 + k] - t[1 + a : 2 + a] * u[b]
    mine = pick(rows, (16, 32))
    four = jnp.concatenate([mine] * 4, axis=1)
    lane = lax.broadcasted_iota(i32, (16, 128), 1)
    part[g] = jnp.where(lane // 32 == lax.rem(g, 4), four, 0.0)
    done(send(part.at[g], part.at[g], across, s3, r3))
    for k in range(4):
        top[s, k] = part[4 * k] + part[4 * k + 1] + part[4 * k + 2] + part[4 * k + 3]
    done(send(top.at[s], top.at[s], within, s4, r4))


def spread(table, pieces, rows):
    at = row_iota((16, 128))
    extra = (at >= 11) & (at < 14)

    def step(k, carry):
        t = table[k]
        h, m, l = split3(t)
        low = pltpu.roll(l, 10, 0)
        both = jnp.concatenate([jnp.where(extra, low, h), jnp.where(extra, 0.0, m)], axis=1)
        pieces[pl.ds(pl.multiple_of(k * 16, 16), 16), :] = both.astype(bf16)
        return carry

    lax.fori_loop(0, rows, step, 0, unroll=4)


def lookup(pieces, rows, row, lane):
    n = row.shape[1]
    hot = jnp.where(row_iota((128, n)) == lane, 1.0, 0.0).astype(bf16)
    hot = jnp.concatenate([hot, hot], axis=0)
    row16 = jnp.broadcast_to(row, (16, n))

    def step(i, got):
        block = pieces[pl.ds(pl.multiple_of(i * 128, 128), 128), :]
        found = dot(block, hot, (1, 0))
        for u in range(8):
            got = jnp.where(row16 == i * 8 + u, found[u * 16 : u * 16 + 16], got)
        return got

    return lax.fori_loop(0, rows // 8, step, jnp.zeros((16, n), f32))


def near_item(load, ids):
    first = load(ids[0])
    is_pos = row_iota((4, WIDE)) < 3
    origin = jnp.where(is_pos, jnp.broadcast_to(first[:, 0:1], (4, WIDE)), 0.0)
    y = first - origin
    h = rnd(y)
    mid = rnd(y - h)
    fine = h + mid
    th, tm, tl = split3(square(fine))
    far_h = jnp.where(is_pos, -2.0 * h, 0.0)
    far_m = jnp.where(is_pos, -2.0 * mid, 0.0)
    one = jnp.ones((1, WIDE), f32)
    ct = pick({0: one, 1: one, 2: one, 3: th, 4: tm, 5: tl}, (8, WIDE))
    target = jnp.concatenate([far_h, far_h, far_m, far_m, ct], axis=0).astype(bf16)
    total = jnp.zeros((16, WIDE), f32)
    for k in range(4):
        raw = first if k == 0 else load(ids[k])
        ys = raw - origin
        sh = rnd(ys)
        sm = rnd(ys - sh)
        sf = sh + sm
        qh, qm, ql = split3(square(sf) + soften)
        cs = pick({0: qh, 1: qm, 2: ql, 3: one, 4: one, 5: one}, (8, WIDE))
        source = jnp.concatenate([sh, sm, sh, sm, cs], axis=0)
        r = lax.rsqrt(dot(source, target, (0, 0)))
        w = (r * r * r).astype(bf16)
        z = jnp.where(is_pos, sf * raw[3:4], raw)
        zh, zm, zl = split3(z)
        left = jnp.concatenate([zh, zm, zl, jnp.zeros((4, WIDE), f32)], axis=0)
        total = total + dot(left, w, (1, 0))
    s = total[0:4] + total[4:8] + total[8:12]
    return s - fine * s[3:4], origin, y


def far_item(cells, origin, y):
    o = [jnp.broadcast_to(origin[i : i + 1, 0:1], (1, 128)) for i in range(3)]
    mass = cells[0:1]
    px, py, pz = [cells[1 + c : 2 + c] + cells[11 + c : 12 + c] - o[c] for c in range(3)]
    trace = cells[4:5] + cells[5:6] + cells[6:7]
    qxx, qyy, qzz = [3.0 * cells[i : i + 1] - trace for i in (4, 5, 6)]
    qxy, qxz, qyz = [3.0 * cells[i : i + 1] for i in (7, 8, 9)]
    gx = qxx * px + qxy * py + qxz * pz
    gy = qxy * px + qyy * py + qyz * pz
    gz = qxz * px + qyz * py + qzz * pz
    one = jnp.ones((1, 128), f32)
    pp = px * px + py * py + pz * pz + soften
    cs = pick({0: pp, 1: -2.0 * px, 2: -2.0 * py, 3: -2.0 * pz, 4: one, 5: one, 6: one}, (16, 128))
    pg = px * gx + py * gy + pz * gz
    cq = pick(
        {0: pg, 1: -2.0 * gx, 2: -2.0 * gy, 3: -2.0 * gz, 4: qxx, 5: qyy, 6: qzz, 7: 2.0 * qxy, 8: 2.0 * qxz, 9: 2.0 * qyz},
        (16, 128),
    )
    c = jnp.concatenate([cs, cq], axis=1)
    a, b, d = y[0:1], y[1:2], y[2:3]
    ones = jnp.ones((1, WIDE), f32)
    phi = pick(
        {0: ones, 1: a, 2: b, 3: d, 4: a * a, 5: b * b, 6: d * d, 7: a * b, 8: a * d, 9: b * d}, (16, WIDE)
    )
    ch, cm, cl = split3(c)
    fh, fm, fl = split3(phi)
    sq = dot(
        jnp.concatenate([ch, ch, cm, cm, ch, cl], axis=0),
        jnp.concatenate([fh, fm, fh, fm, fl, fh], axis=0),
        (0, 0),
    )
    s, q = sq[0:128], sq[128:256]
    r = lax.rsqrt(s)
    r2 = r * r
    r3 = r * r2
    r5 = r3 * r2
    l1 = pick({0: mass * px, 1: mass * py, 2: mass * pz, 3: -mass}, (16, 128))
    l2 = pick({0: 2.5 * px, 1: 2.5 * py, 2: 2.5 * pz, 3: -2.5 * one}, (16, 128))
    l3 = pick({0: -gx, 1: -gy, 2: -gz, 4: qxx, 5: qyy, 6: qzz, 7: qxy, 8: qxz, 9: qyz}, (16, 128))
    out = jnp.zeros((32, WIDE), f32)
    for l, v in ((l1, r3), (l2, q * (r5 * r2)), (l3, r5)):
        lh = rnd(l)
        pieces = jnp.concatenate([lh, rnd(l - lh)], axis=0)
        vh = v.astype(bf16)
        vm = (v - vh.astype(f32)).astype(bf16)
        out = out + dot(
            jnp.concatenate([pieces, pieces], axis=1), jnp.concatenate([vh, vm], axis=0), (1, 0)
        )
    t = out[0:16] + out[16:32]
    axx, ayy, azz, axy, axz, ayz = [t[i : i + 1] for i in range(4, 10)]
    turned = pick(
        {0: axx * a + axy * b + axz * d, 1: axy * a + ayy * b + ayz * d, 2: axz * a + ayz * b + azz * d}, (4, WIDE)
    )
    return t[0:4] + t[3:4] * y + turned


def force_body(near, row, lane, tops, table, top, load, out, pieces, top_pieces, cells):
    spread(table, pieces, SUB * DOM)
    spread(top, top_pieces, 32)

    def gather(i, carry):
        ess = [
            lookup(pieces, SUB * DOM, row[pl.ds(2 * i + u, 1), :], lane[pl.ds(2 * i + u, 1), :])
            for u in range(2)
        ]
        t = tops[pl.ds(i, 1), :]
        far = lookup(top_pieces, 32, t >> 7, t & 127)
        blank = jnp.zeros((16, 32), f32)
        for u in range(8):
            e = ess[u // 4][:, (u % 4) * 64 : (u % 4) * 64 + 64]
            cells[i * 8 + u] = jnp.concatenate([e, far[:, u * 32 : u * 32 + 32], blank], axis=1)
        return carry

    lax.fori_loop(0, ITEMS // 8, gather, 0)

    def item(w, carry):
        acc, origin, y = near_item(load, [near[w * 4 + k] for k in range(4)])
        out[w] = acc + far_item(cells[w], origin, y)
        return carry

    lax.fori_loop(0, ITEMS, item, 0)


def force1_kernel(near, row, lane, tops, table, top, x, out, pieces, top_pieces, cells):
    force_body(near, row, lane, tops, table, top, lambda i: x[i], out, pieces, top_pieces, cells)


def force2_kernel(near, slot, row, lane, tops, table, top, x, ahead, force, out, pieces, top_pieces, cells):
    def load(i):
        p = ahead[i]
        k = slot[i]
        f = jnp.where(k >= 0, force[jnp.maximum(k, 0)], 0.0)
        moved = p + (2.0 * kick * time_step) * p[3:4] * f
        return jnp.where(row_iota((4, WIDE)) < 3, moved, x[i])

    force_body(near, row, lane, tops, table, top, load, out, pieces, top_pieces, cells)


def lists_kernel(ids, codes, row, lane):
    def one(i, carry):
        c = ids[pl.ds(i, 1), :]
        hot = jnp.where(row_iota((128, 256)) == (c & 127), 1.0, 0.0)
        r = dot((codes[...] >> 7).astype(f32), hot, (1, 0))
        l = dot((codes[...] & 127).astype(f32), hot, (1, 0))
        at = row_iota((32, 256)) == (c >> 7)
        row[pl.ds(i, 1), :] = jnp.sum(jnp.where(at, r, 0.0), axis=0, keepdims=True).astype(i32)
        lane[pl.ds(i, 1), :] = jnp.sum(jnp.where(at, l, 0.0), axis=0, keepdims=True).astype(i32)
        return carry

    lax.fori_loop(0, 10, one, 0)


V = pl.BlockSpec(memory_space=pltpu.VMEM)
S = pl.BlockSpec(memory_space=pltpu.SMEM)


def shaped(*shape, dtype=f32):
    return jax.ShapeDtypeStruct(shape, dtype)


def call(kernel, outs, places, scratch, args, **params):
    return pl.pallas_call(
        kernel,
        out_shape=outs,
        in_specs=places,
        out_specs=jax.tree.map(lambda _: V, outs),
        scratch_shapes=scratch,
        compiler_params=pltpu.CompilerParams(vmem_limit_bytes=48 * MIB, **params),
    )(*args)


def exchange_cells(rec):
    dma = pltpu.SemaphoreType.DMA
    return call(
        cells_kernel,
        (shaped(SUB, DOM, 16, 128), shaped(SUB, 4, 16, 128)),
        [V],
        [pltpu.VMEM((DOM, 16, 128), f32), pltpu.VMEM((48, 32), f32)]
        + [dma((DOM - 1,)), dma((DOM - 1,)), dma((SUB - 1,)), dma((SUB - 1,))] * 2,
        (rec,),
        collective_id=1,
        has_side_effects=True,
    )


def body(positions, velocities, masses, accel_prev, active, bucket_top, near_list, cell_list, top_list, essential, work):
    n = positions.shape[1]
    sub_index = lax.axis_index("sub")
    act = active.reshape(1, n)
    mass = masses.reshape(1, n)
    top_row = bucket_top.astype(f32).reshape(1, BUCKETS)

    wanted = essential.reshape(DOM, -1)
    codes = ((wanted >> 7) * DOM + jnp.arange(DOM, dtype=i32)[:, None]) * 128 + (wanted & 127)
    lists = jnp.concatenate([near_list, cell_list, top_list, jnp.zeros((BUCKETS, 28), i32)], axis=1)
    tail = jnp.concatenate([work, jnp.full((128 - ITEMS,), -1, i32)])[None]
    packed = jnp.concatenate([lists, codes.reshape(4, 128), tail, jnp.zeros((3, 128), i32)], axis=0)
    shared = lax.all_gather(packed, "sub", axis=0, tiled=False)
    rows = shared[:, :BUCKETS].reshape(GROUP, 128)[work]
    near = rows[:, :4].reshape(-1)
    tops = rows[:, 68:100].reshape(5, 256)
    row, lane = call(
        lists_kernel, (shaped(10, 256, dtype=i32), shaped(10, 256, dtype=i32)), [V, V], [],
        (rows[:, 4:68].reshape(10, 256), shared[:, BUCKETS : BUCKETS + 4].reshape(32, 128)),
    )
    all_work = shared[:, BUCKETS + 4, :ITEMS].reshape(-1)
    order = jnp.arange(SUB * ITEMS, dtype=i32)
    slot = jnp.max(
        jnp.where(all_work[None, :] == jnp.arange(GROUP, dtype=i32)[:, None], order[None, :], -1), axis=1
    )
    own_slot = lax.dynamic_slice(slot, (sub_index * BUCKETS,), (BUCKETS,))

    flat, boxed = shaped(3, n), shaped(BUCKETS, 4, WIDE)
    record = shaped(16, BUCKETS)
    dense = [pltpu.VMEM((4, BUCKETS, WIDE), f32)]
    half, x4, p4, rec = call(
        first_kernel, (flat, boxed, boxed, record), [V] * 6, dense,
        (positions, velocities, accel_prev, act, mass, top_row),
    )
    x = lax.all_gather(x4, "sub", axis=0, tiled=True)
    ahead = lax.all_gather(p4, "sub", axis=0, tiled=True)

    scratch = [
        pltpu.VMEM((SUB * DOM * 16, 256), bf16),
        pltpu.VMEM((32 * 16, 256), bf16),
        pltpu.VMEM((ITEMS, 16, 128), f32),
    ]

    def tables(rec):
        table, top = exchange_cells(rec)
        return table.reshape(SUB * DOM, 16, 128), top.reshape(32, 16, 128)

    acc = call(
        force1_kernel, shaped(ITEMS, 4, WIDE), [S] + [V] * 6, scratch, (near, row, lane, tops, *tables(rec), x)
    )
    force = lax.all_gather(acc, "sub", axis=0, tiled=True)
    half, places, rec = call(
        second_kernel, (flat, flat, record), [S] + [V] * 6, dense, (own_slot, x4, half, act, mass, top_row, force)
    )
    acc = call(
        force2_kernel, shaped(ITEMS, 4, WIDE), [S, S] + [V] * 8, scratch,
        (near, slot, row, lane, tops, *tables(rec), x, ahead, force),
    )
    force = lax.all_gather(acc, "sub", axis=0, tiled=True)
    speeds = call(last_kernel, flat, [S] + [V] * 3, [], (own_slot, half, act, force))
    return (speeds, places)


def solution(mesh):
    both = ("dom", "sub")
    in_specs = (
        P(None, both), P(None, both), P(both), P(None, both), P(both), P(both),
        P(both, None), P(both, None), P(both, None), P("dom", "sub", None, None), P(both),
    )
    return jax.shard_map(
        body, mesh=mesh, in_specs=in_specs, out_specs=(P(None, both), P(None, both)), check_vma=False
    )
```

```python
import jax
import jax.numpy as jnp
from jax import lax
from jax.experimental import pallas as pl
from jax.experimental.pallas import tpu as pltpu
from jax.sharding import PartitionSpec as P

f32, bf16, i32 = jnp.float32, jnp.bfloat16, jnp.int32
MESH = pl.DeviceIdType.MESH
SUB, DOM = 8, 16
BUCKETS, WIDE, ITEMS = 128, 256, 40
GROUP = SUB * BUCKETS
TOP_SIDE = 16
MIB = 2**20

time_step = 0.01
soften = 0.0025
mass_floor = 0.5
kick = 0.5 * time_step
PAIRS = ((0, 0), (1, 1), (2, 2), (0, 1), (0, 2), (1, 2))
NEAR_1, NEAR_2, NEAR_3, NEAR_4 = 8, 20, 28, 36


def rnd(a):
    return a.astype(bf16).astype(f32)


def split3(a):
    h = rnd(a)
    r = a - h
    m = rnd(r)
    return h, m, rnd(r - m)


def dot(a, b, dims):
    return lax.dot_general(
        a.astype(bf16), b.astype(bf16), ((dims[:1], dims[1:]), ((), ())), preferred_element_type=f32
    )


def row_iota(shape):
    return lax.broadcasted_iota(i32, shape, 0)


def pick(rows, shape):
    at = row_iota(shape)
    out = jnp.zeros(shape, f32)
    for i, v in rows.items():
        out = jnp.where(at == i, v, out)
    return out


def square(y):
    q = y * y
    return q[0:1] + q[1:2] + q[2:3]


def moments(dense, top_row, rec_ref):
    first = [dense[c][:, 0:1] for c in range(3)]
    y = [dense[c] - first[c] for c in range(3)]
    m = dense[3]
    ones = jnp.ones((8, WIDE), f32)
    lead = jnp.where(lax.broadcasted_iota(i32, (8, WIDE), 1) == 0, 1.0, 0.0)

    def total(a, by=ones):
        return lax.dot_general(
            by, a, (((1,), (1,)), ((), ())), precision=lax.Precision.HIGHEST, preferred_element_type=f32
        )[0:1]

    my = [m * y[c] for c in range(3)]
    mass = total(m)
    start = [total(dense[c], lead) for c in range(3)]
    s = [total(my[c]) for c in range(3)]
    d = [s[c] / mass for c in range(3)]
    second = [total(my[a] * y[b]) - s[a] * d[b] for a, b in PAIRS]
    rows = {0: mass, 10: top_row}
    for c in range(3):
        rows[1 + c] = start[c] + d[c]
    for k in range(6):
        rows[4 + k] = second[k]
    rec_ref[...] = pick(rows, (16, BUCKETS))


def first_kernel(pos, vel, acc, act, mass, top_row, half_ref, x4_ref, p4_ref, rec_ref, dense):
    def one(b, carry):
        sl = pl.ds(pl.multiple_of(b * WIDE, WIDE), WIDE)
        a = act[:, sl].astype(f32)
        h = vel[:, sl] + kick * a * acc[:, sl]
        x = pos[:, sl] + time_step * h
        half_ref[:, sl] = h
        m = mass[:, sl]
        x4_ref[b] = jnp.concatenate([x, m], axis=0)
        p4_ref[b] = jnp.concatenate([x + time_step * h, a], axis=0)
        for c in range(3):
            dense[c, pl.ds(b, 1), :] = x[c : c + 1]
        dense[3, pl.ds(b, 1), :] = m
        return carry

    lax.fori_loop(0, BUCKETS, one, 0, unroll=4)
    moments(dense, top_row[...], rec_ref)


def second_kernel(slot, x4, half, act, mass, top_row, force, half_ref, pos_ref, rec_ref, dense):
    def one(b, carry):
        sl = pl.ds(pl.multiple_of(b * WIDE, WIDE), WIDE)
        a = act[:, sl].astype(f32)
        f = forced(force, slot[b])
        push = kick * a * f
        h = half[:, sl] + push + push
        x = x4[b][0:3] + time_step * h
        half_ref[:, sl] = h
        pos_ref[:, sl] = x
        for c in range(3):
            dense[c, pl.ds(b, 1), :] = x[c : c + 1]
        dense[3, pl.ds(b, 1), :] = mass[:, sl]
        return carry

    lax.fori_loop(0, BUCKETS, one, 0, unroll=4)
    moments(dense, top_row[...], rec_ref)


def last_kernel(slot, half, act, force, vel_ref):
    def one(b, carry):
        sl = pl.ds(pl.multiple_of(b * WIDE, WIDE), WIDE)
        f = forced(force, slot[b])
        vel_ref[:, sl] = half[:, sl] + kick * act[:, sl].astype(f32) * f
        return carry

    lax.fori_loop(0, BUCKETS, one, 0, unroll=4)


def centre(ids):
    return [
        (part.astype(f32) + 0.5) / TOP_SIDE
        for part in (ids >> 8, (ids >> 4) & 15, ids & 15)
    ]


def spread(table, pieces, rows):
    at = row_iota((16, 128))
    extra = (at >= 11) & (at < 14)

    def step(k, carry):
        t = table(k)
        h, m, l = split3(t)
        low = pltpu.roll(l, 10, 0)
        both = jnp.concatenate([jnp.where(extra, low, h), jnp.where(extra, 0.0, m)], axis=1)
        pieces[pl.ds(pl.multiple_of(k * 16, 16), 16), :] = both.astype(bf16)
        return carry

    lax.fori_loop(0, rows, step, 0, unroll=4)


def lookup(pieces, rows, row, lane):
    n = row.shape[1]
    hot = jnp.where(row_iota((128, n)) == lane, 1.0, 0.0).astype(bf16)
    hot = jnp.concatenate([hot, hot], axis=0)
    row16 = jnp.broadcast_to(row, (16, n))

    def step(i, got):
        block = pieces[pl.ds(pl.multiple_of(i * 128, 128), 128), :]
        found = dot(block, hot, (1, 0))
        for u in range(8):
            got = jnp.where(row16 == i * 8 + u, found[u * 16 : u * 16 + 16], got)
        return got

    return lax.fori_loop(0, rows // 8, step, jnp.zeros((16, n), f32), unroll=rows // 8)


def from_first(first):
    is_pos = row_iota((4, WIDE)) < 3
    origin = jnp.where(is_pos, jnp.broadcast_to(first[:, 0:1], (4, WIDE)), 0.0)
    return is_pos, origin, first - origin


def near_item(load, ids):
    first = load(ids[0])
    is_pos, origin, y = from_first(first)
    h = rnd(y)
    mid = rnd(y - h)
    fine = h + mid
    th, tm, tl = split3(square(fine))
    far_h = jnp.where(is_pos, -2.0 * h, 0.0)
    far_m = jnp.where(is_pos, -2.0 * mid, 0.0)
    one = jnp.ones((1, WIDE), f32)
    ct = pick({0: one, 1: one, 2: one, 3: th, 4: tm, 5: tl}, (8, WIDE))
    target = jnp.concatenate([far_h, far_h, far_m, far_m, ct], axis=0).astype(bf16)
    total = jnp.zeros((WIDE, 16), f32)
    for k in range(4):
        raw = first if k == 0 else load(ids[k])
        ys = raw - origin
        sh = rnd(ys)
        sm = rnd(ys - sh)
        sf = sh + sm
        qh, qm, ql = split3(square(sf) + soften)
        cs = pick({0: qh, 1: qm, 2: ql, 3: one, 4: one, 5: one}, (8, WIDE))
        source = jnp.concatenate([sh, sm, sh, sm, cs], axis=0)
        r = lax.rsqrt(dot(target, source, (0, 0)))
        w = (r * r * r).astype(bf16)
        z = jnp.where(is_pos, sf * raw[3:4], raw)
        zh, zm, zl = split3(z)
        left = jnp.concatenate([zh, zm, zl, jnp.zeros((4, WIDE), f32)], axis=0)
        total = total + dot(w, left, (1, 1))
    total = total.T
    s = total[0:4] + total[4:8] + total[8:12]
    return s - fine * s[3:4]


def far_item(cells, origin, y):
    o = [jnp.broadcast_to(origin[i : i + 1, 0:1], (1, 128)) for i in range(3)]
    mass = cells[0:1]
    px, py, pz = [cells[1 + c : 2 + c] + cells[11 + c : 12 + c] - o[c] for c in range(3)]
    trace = cells[4:5] + cells[5:6] + cells[6:7]
    qxx, qyy, qzz = [3.0 * cells[i : i + 1] - trace for i in (4, 5, 6)]
    qxy, qxz, qyz = [3.0 * cells[i : i + 1] for i in (7, 8, 9)]
    gx = qxx * px + qxy * py + qxz * pz
    gy = qxy * px + qyy * py + qyz * pz
    gz = qxz * px + qyz * py + qzz * pz
    one = jnp.ones((1, 128), f32)
    pp = px * px + py * py + pz * pz + soften
    cs = pick({0: pp, 1: -2.0 * px, 2: -2.0 * py, 3: -2.0 * pz, 4: one, 5: one, 6: one}, (16, 128))
    pg = px * gx + py * gy + pz * gz
    cq = pick(
        {0: pg, 1: -2.0 * gx, 2: -2.0 * gy, 3: -2.0 * gz, 4: qxx, 5: qyy, 6: qzz, 7: 2.0 * qxy, 8: 2.0 * qxz, 9: 2.0 * qyz},
        (16, 128),
    )
    c = jnp.concatenate([cs, cq], axis=1)
    a, b, d = y[0:1], y[1:2], y[2:3]
    ones = jnp.ones((1, WIDE), f32)
    phi = pick(
        {0: ones, 1: a, 2: b, 3: d, 4: a * a, 5: b * b, 6: d * d, 7: a * b, 8: a * d, 9: b * d}, (16, WIDE)
    )
    ch, cm, cl = split3(c)
    fh, fm, fl = split3(phi)
    sq = dot(
        jnp.concatenate([ch, ch, cm, cm, ch, cl], axis=0),
        jnp.concatenate([fh, fm, fh, fm, fl, fh], axis=0),
        (0, 0),
    )
    s, q = sq[0:128], sq[128:256]
    r = lax.rsqrt(s)
    r2 = r * r
    r3 = r * r2
    r5 = r3 * r2
    l1 = pick({0: mass * px, 1: mass * py, 2: mass * pz, 3: -mass}, (16, 128))
    l2 = pick({0: 2.5 * px, 1: 2.5 * py, 2: 2.5 * pz, 3: -2.5 * one}, (16, 128))
    l3 = pick({0: -gx, 1: -gy, 2: -gz, 4: qxx, 5: qyy, 6: qzz, 7: qxy, 8: qxz, 9: qyz}, (16, 128))
    out = jnp.zeros((32, WIDE), f32)
    for l, v in ((l1, r3), (l2, q * (r5 * r2)), (l3, r5)):
        lh = rnd(l)
        pieces = jnp.concatenate([lh, rnd(l - lh)], axis=0)
        vh = v.astype(bf16)
        vm = (v - vh.astype(f32)).astype(bf16)
        out = out + dot(
            jnp.concatenate([pieces, pieces], axis=1), jnp.concatenate([vh, vm], axis=0), (1, 0)
        )
    t = out[0:16] + out[16:32]
    axx, ayy, azz, axy, axz, ayz = [t[i : i + 1] for i in range(4, 10)]
    turned = pick(
        {0: axx * a + axy * b + axz * d, 1: axy * a + ayy * b + ayz * d, 2: axz * a + ayz * b + azz * d}, (4, WIDE)
    )
    return t[0:4] + t[3:4] * y + turned


def top_values(t, ids):
    mass = t[0:1]
    own = t[10:11].astype(i32)
    d = [t[1 + c : 2 + c] - at for c, at in enumerate(centre(own))]
    md = [mass * d[c] for c in range(3)]
    rows = {0: mass, 1: md[0], 2: md[1], 3: md[2]}
    for k, (a, b) in enumerate(PAIRS):
        rows[4 + k] = t[4 + k : 5 + k] + md[a] * d[b]
    pieces = jnp.concatenate(split3(pick(rows, (16, BUCKETS))), axis=0)
    return pieces, jnp.where(ids == own, 1.0, 0.0)


def top_record(t, base):
    mass = t[0:1]
    w = jnp.maximum(mass, mass_floor)
    at = centre(lax.broadcasted_iota(i32, (1, 32), 1) + base)
    u = [t[1 + c : 2 + c] / w for c in range(3)]
    rows = {0: mass}
    for c in range(3):
        rows[1 + c] = at[c] + u[c]
    for k, (a, b) in enumerate(PAIRS):
        rows[4 + k] = t[4 + k : 5 + k] - t[1 + a : 2 + a] * u[b]
    return pick(rows, (16, 32))


def substep(near, row, lane, tops, rec, load, out, scratch):
    (table, top, part, sums, pieces, top_pieces, cells, pairs, s1, r1, s2, r2, s3, r3, s4, r4, s5, r5, s6, r6, s7, r7) = scratch
    g, s = lax.axis_index("dom"), lax.axis_index("sub")
    core, chip = lax.rem(s, 2), s // 2
    sibling = [(g, s + 1 - 2 * core)]
    across = [(lax.rem(g + k, DOM), s) for k in range(1, DOM)]
    within = [(g, lax.rem(s + k, SUB)) for k in range(1, SUB)]
    along = [(g, lax.rem(s + k, SUB)) for k in (2, 6, 4)]
    barrier = pltpu.get_barrier_semaphore()
    for peer in across + within:
        pl.semaphore_signal(barrier, inc=1, device_id=peer, device_id_type=MESH)
    pl.semaphore_wait(barrier, DOM + SUB - 2)

    def send(ref_from, ref_to, peers, sends, recvs):
        copies = [
            pltpu.make_async_remote_copy(
                src_ref=ref_from, dst_ref=ref_to, send_sem=sends.at[k], recv_sem=recvs.at[k],
                device_id=peer, device_id_type=MESH,
            )
            for k, peer in enumerate(peers)
        ]
        for c in copies:
            c.start()
        return copies

    def done(copies):
        for c in copies:
            c.wait()

    def near_part(begin, end):
        def item(w, carry):
            pairs[w] = near_item(load, [near[w * 4 + k] for k in range(4)])
            return carry

        lax.fori_loop(begin, end, item, 0, unroll=4)

    table[core, chip, g] = rec[...]
    flight = send(rec, table.at[core, chip, g], across, s1, r1)
    near_part(0, NEAR_1)
    done(flight)
    flight = send(table.at[core, chip], table.at[core, chip], along, s2, r2)
    near_part(NEAR_1, NEAR_2)
    done(flight)
    flight = send(table.at[core], table.at[core], sibling, s3, r3)
    near_part(NEAR_2, NEAR_3)
    done(flight)

    base = (s * DOM + g) * 32
    ids = lax.broadcasted_iota(i32, (32, BUCKETS), 0) + base
    sums[...] = jnp.zeros_like(sums)

    def step(i, carry):
        at, k = i // 4, (i % 4) * 4
        got = [top_values(table[at // 4, at % 4, k + u], ids) for u in range(4)]
        v = jnp.concatenate([a for a, _ in got], axis=1)
        o = jnp.concatenate([b for _, b in got], axis=1)
        sums[...] += dot(v, o, (1, 1))
        return carry

    lax.fori_loop(0, SUB * DOM // 4, step, 0, unroll=4)
    mine = top_record(sums[0:16] + sums[16:32] + sums[32:48], base)
    four = jnp.concatenate([mine] * 4, axis=1)
    quarter = lax.broadcasted_iota(i32, (16, 128), 1) // 32
    part[g] = jnp.where(quarter == lax.rem(g, 4), four, 0.0)
    flight = send(part.at[g], part.at[g], across, s4, r4)
    near_part(NEAR_3, NEAR_4)
    done(flight)
    for k in range(4):
        top[s, k] = part[4 * k] + part[4 * k + 1] + part[4 * k + 2] + part[4 * k + 3]
    flight = send(top.at[s], top.at[s], within, s5, r5)

    spread(lambda k: table[k // 64, k // 16 % 4, k % 16], pieces, SUB * DOM)

    def gather(i, carry):
        ess = lookup(pieces, SUB * DOM, row[pl.ds(i, 1), :], lane[pl.ds(i, 1), :])
        blank = jnp.zeros((16, 64), f32)
        for u in range(4):
            cells[i * 4 + u] = jnp.concatenate([ess[:, u * 64 : u * 64 + 64], blank], axis=1)
        return carry

    lax.fori_loop(0, ITEMS // 4, gather, 0)
    near_part(NEAR_4, ITEMS)
    done(flight)
    spread(lambda k: top[k // 4, k % 4], top_pieces, 32)

    def gather_top(i, carry):
        t = tops[pl.ds(i, 1), :]
        far = lookup(top_pieces, 32, t >> 7, t & 127)
        blank = [jnp.zeros((16, n), f32) for n in (64, 32)]
        for u in range(8):
            cells[i * 8 + u] += jnp.concatenate([blank[0], far[:, u * 32 : u * 32 + 32], blank[1]], axis=1)
        return carry

    lax.fori_loop(0, ITEMS // 8, gather_top, 0)

    def item(w, carry):
        _, origin, y = from_first(load(near[w * 4]))
        acc = pairs[w] + far_item(cells[w], origin, y)
        for c in range(3):
            out[core, chip, c, pl.ds(w, 1), :] = acc[c : c + 1]
        return carry

    lax.fori_loop(0, ITEMS, item, 0, unroll=4)
    done(send(out.at[core, chip], out.at[core, chip], along, s6, r6))
    done(send(out.at[core], out.at[core], sibling, s7, r7))


def substep1_kernel(near, row, lane, tops, rec, x, out, *scratch):
    substep(near, row, lane, tops, rec, lambda i: x[i], out, scratch)


def forced(force, slot):
    k = jnp.maximum(slot, 0)
    block, w = k // ITEMS, lax.rem(k, ITEMS)
    rows = [force[block // 4, lax.rem(block, 4), c, pl.ds(w, 1), :] for c in range(3)]
    return jnp.where(slot >= 0, jnp.concatenate(rows, axis=0), 0.0)


def substep2_kernel(near, slot, row, lane, tops, rec, x, ahead, force, out, *scratch):
    def load(i):
        p = ahead[i]
        old = x[i]
        moved = p[0:3] + (2.0 * kick * time_step) * p[3:4] * forced(force, slot[i])
        return jnp.concatenate([moved, old[3:4]], axis=0)

    substep(near, row, lane, tops, rec, load, out, scratch)


def lists_kernel(ids, codes, row, lane):
    def one(i, carry):
        c = ids[pl.ds(i, 1), :]
        hot = jnp.where(row_iota((128, 256)) == (c & 127), 1.0, 0.0)
        r = dot((codes[...] >> 7).astype(f32), hot, (1, 0))
        l = dot((codes[...] & 127).astype(f32), hot, (1, 0))
        at = row_iota((32, 256)) == (c >> 7)
        row[pl.ds(i, 1), :] = jnp.sum(jnp.where(at, r, 0.0), axis=0, keepdims=True).astype(i32)
        lane[pl.ds(i, 1), :] = jnp.sum(jnp.where(at, l, 0.0), axis=0, keepdims=True).astype(i32)
        return carry

    lax.fori_loop(0, 10, one, 0)


V = pl.BlockSpec(memory_space=pltpu.VMEM)
S = pl.BlockSpec(memory_space=pltpu.SMEM)


def shaped(*shape, dtype=f32):
    return jax.ShapeDtypeStruct(shape, dtype)


def call(kernel, outs, places, scratch, args, **params):
    return pl.pallas_call(
        kernel,
        out_shape=outs,
        in_specs=places,
        out_specs=jax.tree.map(lambda _: V, outs),
        scratch_shapes=scratch,
        compiler_params=pltpu.CompilerParams(vmem_limit_bytes=48 * MIB, **params),
    )(*args)


def exchange(kernel, places, args, collective_id):
    peers = (DOM - 1, 3, 1, DOM - 1, SUB - 1, 3, 1)
    scratch = [
        pltpu.VMEM((2, SUB // 2, DOM, 16, 128), f32),
        pltpu.VMEM((SUB, 4, 16, 128), f32),
        pltpu.VMEM((DOM, 16, 128), f32),
        pltpu.VMEM((48, 32), f32),
        pltpu.VMEM((SUB * DOM * 16, 256), bf16),
        pltpu.VMEM((32 * 16, 256), bf16),
        pltpu.VMEM((ITEMS, 16, 128), f32),
        pltpu.VMEM((ITEMS, 4, WIDE), f32),
    ]
    for n in peers:
        scratch += [pltpu.SemaphoreType.DMA((n,))] * 2
    return call(
        kernel, shaped(2, SUB // 2, 3, ITEMS, WIDE), places, scratch, args,
        collective_id=collective_id, has_side_effects=True,
    )


def by_core(s):
    return (s & 1) * (SUB // 2) + (s >> 1)


def body(positions, velocities, masses, accel_prev, active, bucket_top, near_list, cell_list, top_list, essential, work):
    n = positions.shape[1]
    sub_index = lax.axis_index("sub")
    act = active.reshape(1, n)
    mass = masses.reshape(1, n)
    top_row = bucket_top.astype(f32).reshape(1, BUCKETS)

    wanted = essential.reshape(DOM, -1)
    device = by_core(wanted >> 7)
    codes = (device * DOM + jnp.arange(DOM, dtype=i32)[:, None]) * 128 + (wanted & 127)
    lists = jnp.concatenate([near_list, cell_list, top_list, jnp.zeros((BUCKETS, 28), i32)], axis=1)
    tail = jnp.concatenate([work, jnp.full((128 - ITEMS,), -1, i32)])[None]
    packed = jnp.concatenate([lists, codes.reshape(4, 128), tail, jnp.zeros((3, 128), i32)], axis=0)
    shared = lax.all_gather(packed, "sub", axis=0, tiled=False)
    rows = shared[:, :BUCKETS].reshape(GROUP, 128)[work]
    near = rows[:, :4].reshape(-1)
    tops = rows[:, 68:100].reshape(5, 256)
    row, lane = call(
        lists_kernel, (shaped(10, 256, dtype=i32), shaped(10, 256, dtype=i32)), [V, V], [],
        (rows[:, 4:68].reshape(10, 256), shared[:, BUCKETS : BUCKETS + 4].reshape(32, 128)),
    )
    all_work = shared[:, BUCKETS + 4, :ITEMS].reshape(-1)
    order = jnp.arange(SUB * ITEMS, dtype=i32)
    order = by_core(order // ITEMS) * ITEMS + order % ITEMS
    slot = jnp.max(
        jnp.where(all_work[None, :] == jnp.arange(GROUP, dtype=i32)[:, None], order[None, :], -1), axis=1
    )
    own_slot = lax.dynamic_slice(slot, (sub_index * BUCKETS,), (BUCKETS,))

    flat, boxed = shaped(3, n), shaped(BUCKETS, 4, WIDE)
    record = shaped(16, BUCKETS)
    dense = [pltpu.VMEM((4, BUCKETS, WIDE), f32)]
    half, x4, p4, rec = call(
        first_kernel, (flat, boxed, boxed, record), [V] * 6, dense,
        (positions, velocities, accel_prev, act, mass, top_row),
    )
    x = lax.all_gather(x4, "sub", axis=0, tiled=True)
    ahead = lax.all_gather(p4, "sub", axis=0, tiled=True)

    force = exchange(substep1_kernel, [S] + [V] * 5, (near, row, lane, tops, rec, x), 1)
    half, places, rec = call(
        second_kernel, (flat, flat, record), [S] + [V] * 6, dense, (own_slot, x4, half, act, mass, top_row, force)
    )
    force = exchange(
        substep2_kernel, [S, S] + [V] * 7, (near, slot, row, lane, tops, rec, x, ahead, force), 2
    )
    speeds = call(last_kernel, flat, [S] + [V] * 3, [], (own_slot, half, act, force))
    return (speeds, places)


def solution(mesh):
    both = ("dom", "sub")
    in_specs = (
        P(None, both), P(None, both), P(both), P(None, both), P(both), P(both),
        P(both, None), P(both, None), P(both, None), P("dom", "sub", None, None), P(both),
    )
    return jax.shard_map(
        body, mesh=mesh, in_specs=in_specs, out_specs=(P(None, both), P(None, both)), check_vma=False
    )
```

```python
import jax
import jax.numpy as jnp
from jax import lax
from jax.experimental import pallas as pl
from jax.experimental.pallas import tpu as pltpu
from jax.sharding import PartitionSpec as P

f32, bf16, i32 = jnp.float32, jnp.bfloat16, jnp.int32
MESH = pl.DeviceIdType.MESH
SUB, DOM = 8, 16
BUCKETS, WIDE, ITEMS = 128, 256, 40
GROUP = SUB * BUCKETS
TOP_SIDE = 16
MIB = 2**20

time_step = 0.01
soften = 0.0025
mass_floor = 0.5
kick = 0.5 * time_step
PAIRS = ((0, 0), (1, 1), (2, 2), (0, 1), (0, 2), (1, 2))
NEAR_AT = 96
COPIES = 128


def rnd(a):
    return a.astype(bf16).astype(f32)


def split3(a):
    h = rnd(a)
    r = a - h
    m = rnd(r)
    return h, m, rnd(r - m)


def dot(a, b, dims):
    return lax.dot_general(
        a.astype(bf16), b.astype(bf16), ((dims[:1], dims[1:]), ((), ())), preferred_element_type=f32
    )


def row_iota(shape):
    return lax.broadcasted_iota(i32, shape, 0)


def pick(rows, shape):
    at = row_iota(shape)
    out = jnp.zeros(shape, f32)
    for i, v in rows.items():
        out = jnp.where(at == i, v, out)
    return out


def square(y):
    q = y * y
    return q[0:1] + q[1:2] + q[2:3]


def moments(dense, top_row, rec_ref):
    first = [dense[c][:, 0:1] for c in range(3)]
    y = [dense[c] - first[c] for c in range(3)]
    m = dense[3]
    ones = jnp.ones((8, WIDE), f32)
    lead = jnp.where(lax.broadcasted_iota(i32, (8, WIDE), 1) == 0, 1.0, 0.0)

    def total(a, by=ones):
        return lax.dot_general(
            by, a, (((1,), (1,)), ((), ())), precision=lax.Precision.HIGHEST, preferred_element_type=f32
        )[0:1]

    my = [m * y[c] for c in range(3)]
    mass = total(m)
    start = [total(dense[c], lead) for c in range(3)]
    s = [total(my[c]) for c in range(3)]
    d = [s[c] / mass for c in range(3)]
    second = [total(my[a] * y[b]) - s[a] * d[b] for a, b in PAIRS]
    rows = {0: mass, 10: top_row}
    for c in range(3):
        rows[1 + c] = start[c] + d[c]
    for k in range(6):
        rows[4 + k] = second[k]
    rec_ref[...] = pick(rows, (16, BUCKETS))


def centre(ids):
    return [
        (part.astype(f32) + 0.5) / TOP_SIDE
        for part in (ids >> 8, (ids >> 4) & 15, ids & 15)
    ]


def spread(table, pieces, rows):
    at = row_iota((16, 128))
    extra = (at >= 11) & (at < 14)

    def step(k, carry):
        t = table(k)
        h, m, l = split3(t)
        low = pltpu.roll(l, 10, 0)
        both = jnp.concatenate([jnp.where(extra, low, h), jnp.where(extra, 0.0, m)], axis=1)
        pieces[pl.ds(pl.multiple_of(k * 16, 16), 16), :] = both.astype(bf16)
        return carry

    lax.fori_loop(0, rows, step, 0, unroll=4)


def lookup(pieces, rows, row, lane):
    n = row.shape[1]
    hot = jnp.where(row_iota((128, n)) == lane, 1.0, 0.0).astype(bf16)
    hot = jnp.concatenate([hot, hot], axis=0)
    row16 = jnp.broadcast_to(row, (16, n))

    def step(i, got):
        block = pieces[pl.ds(pl.multiple_of(i * 128, 128), 128), :]
        found = dot(block, hot, (1, 0))
        for u in range(8):
            got = jnp.where(row16 == i * 8 + u, found[u * 16 : u * 16 + 16], got)
        return got

    return lax.fori_loop(0, rows // 8, step, jnp.zeros((16, n), f32), unroll=rows // 8)


def from_first(first):
    is_pos = row_iota((4, WIDE)) < 3
    origin = jnp.where(is_pos, jnp.broadcast_to(first[:, 0:1], (4, WIDE)), 0.0)
    return is_pos, origin, first - origin


def near_item(load, ids):
    first = load(ids[0])
    is_pos, origin, y = from_first(first)
    h = rnd(y)
    mid = rnd(y - h)
    fine = h + mid
    th, tm, tl = split3(square(fine))
    far_h = jnp.where(is_pos, -2.0 * h, 0.0)
    far_m = jnp.where(is_pos, -2.0 * mid, 0.0)
    one = jnp.ones((1, WIDE), f32)
    ct = pick({0: one, 1: one, 2: one, 3: th, 4: tm, 5: tl}, (8, WIDE))
    target = jnp.concatenate([far_h, far_h, far_m, far_m, ct], axis=0).astype(bf16)
    total = jnp.zeros((WIDE, 16), f32)
    for k in range(4):
        raw = first if k == 0 else load(ids[k])
        ys = raw - origin
        sh = rnd(ys)
        sm = rnd(ys - sh)
        sf = sh + sm
        qh, qm, ql = split3(square(sf) + soften)
        cs = pick({0: qh, 1: qm, 2: ql, 3: one, 4: one, 5: one}, (8, WIDE))
        source = jnp.concatenate([sh, sm, sh, sm, cs], axis=0)
        r = lax.rsqrt(dot(target, source, (0, 0)))
        w = (r * r * r).astype(bf16)
        z = jnp.where(is_pos, sf * raw[3:4], raw)
        zh, zm, zl = split3(z)
        left = jnp.concatenate([zh, zm, zl, jnp.zeros((4, WIDE), f32)], axis=0)
        total = total + dot(w, left, (1, 1))
    total = total.T
    s = total[0:4] + total[4:8] + total[8:12]
    return s - fine * s[3:4]


def far_item(cells, origin, y):
    o = [jnp.broadcast_to(origin[i : i + 1, 0:1], (1, 128)) for i in range(3)]
    mass = cells[0:1]
    px, py, pz = [cells[1 + c : 2 + c] + cells[11 + c : 12 + c] - o[c] for c in range(3)]
    trace = cells[4:5] + cells[5:6] + cells[6:7]
    qxx, qyy, qzz = [3.0 * cells[i : i + 1] - trace for i in (4, 5, 6)]
    qxy, qxz, qyz = [3.0 * cells[i : i + 1] for i in (7, 8, 9)]
    gx = qxx * px + qxy * py + qxz * pz
    gy = qxy * px + qyy * py + qyz * pz
    gz = qxz * px + qyz * py + qzz * pz
    one = jnp.ones((1, 128), f32)
    pp = px * px + py * py + pz * pz + soften
    cs = pick({0: pp, 1: -2.0 * px, 2: -2.0 * py, 3: -2.0 * pz, 4: one, 5: one, 6: one}, (16, 128))
    pg = px * gx + py * gy + pz * gz
    cq = pick(
        {0: pg, 1: -2.0 * gx, 2: -2.0 * gy, 3: -2.0 * gz, 4: qxx, 5: qyy, 6: qzz, 7: 2.0 * qxy, 8: 2.0 * qxz, 9: 2.0 * qyz},
        (16, 128),
    )
    c = jnp.concatenate([cs, cq], axis=1)
    a, b, d = y[0:1], y[1:2], y[2:3]
    ones = jnp.ones((1, WIDE), f32)
    phi = pick(
        {0: ones, 1: a, 2: b, 3: d, 4: a * a, 5: b * b, 6: d * d, 7: a * b, 8: a * d, 9: b * d}, (16, WIDE)
    )
    ch, cm, cl = split3(c)
    fh, fm, fl = split3(phi)
    sq = dot(
        jnp.concatenate([ch, ch, cm, cm, ch, cl], axis=0),
        jnp.concatenate([fh, fm, fh, fm, fl, fh], axis=0),
        (0, 0),
    )
    s, q = sq[0:128], sq[128:256]
    r = lax.rsqrt(s)
    r2 = r * r
    r3 = r * r2
    r5 = r3 * r2
    l1 = pick({0: mass * px, 1: mass * py, 2: mass * pz, 3: -mass}, (16, 128))
    l2 = pick({0: 2.5 * px, 1: 2.5 * py, 2: 2.5 * pz, 3: -2.5 * one}, (16, 128))
    l3 = pick({0: -gx, 1: -gy, 2: -gz, 4: qxx, 5: qyy, 6: qzz, 7: qxy, 8: qxz, 9: qyz}, (16, 128))
    out = jnp.zeros((32, WIDE), f32)
    for l, v in ((l1, r3), (l2, q * (r5 * r2)), (l3, r5)):
        lh = rnd(l)
        pieces = jnp.concatenate([lh, rnd(l - lh)], axis=0)
        vh = v.astype(bf16)
        vm = (v - vh.astype(f32)).astype(bf16)
        out = out + dot(
            jnp.concatenate([pieces, pieces], axis=1), jnp.concatenate([vh, vm], axis=0), (1, 0)
        )
    t = out[0:16] + out[16:32]
    axx, ayy, azz, axy, axz, ayz = [t[i : i + 1] for i in range(4, 10)]
    turned = pick(
        {0: axx * a + axy * b + axz * d, 1: axy * a + ayy * b + ayz * d, 2: axz * a + ayz * b + azz * d}, (4, WIDE)
    )
    return t[0:4] + t[3:4] * y + turned


def top_values(t, ids):
    mass = t[0:1]
    own = t[10:11].astype(i32)
    d = [t[1 + c : 2 + c] - at for c, at in enumerate(centre(own))]
    md = [mass * d[c] for c in range(3)]
    rows = {0: mass, 1: md[0], 2: md[1], 3: md[2]}
    for k, (a, b) in enumerate(PAIRS):
        rows[4 + k] = t[4 + k : 5 + k] + md[a] * d[b]
    pieces = jnp.concatenate(split3(pick(rows, (16, BUCKETS))), axis=0)
    return pieces, jnp.where(ids == own, 1.0, 0.0)


def top_record(t, base):
    mass = t[0:1]
    w = jnp.maximum(mass, mass_floor)
    at = centre(lax.broadcasted_iota(i32, (1, 32), 1) + base)
    u = [t[1 + c : 2 + c] / w for c in range(3)]
    rows = {0: mass}
    for c in range(3):
        rows[1 + c] = at[c] + u[c]
    for k, (a, b) in enumerate(PAIRS):
        rows[4 + k] = t[4 + k : 5 + k] - t[1 + a : 2 + a] * u[b]
    return pick(rows, (16, 32))


def forced(force, slot):
    k = jnp.maximum(slot, 0)
    block, w = k // ITEMS, lax.rem(k, ITEMS)
    rows = [force[block // 4, lax.rem(block, 4), c, pl.ds(w, 1), :] for c in range(3)]
    return jnp.where(slot >= 0, jnp.concatenate(rows, axis=0), 0.0)


def kernel(
    work, pos_in, vel_in, acc_in, act_in, mass_in, top_row, packed,
    vel_out, pos_out,
    pos, vel, acc, act, mass, half, dense, x, ahead,
    table_1, top_1, part_1, force_1, table_2, top_2, part_2, force_2,
    sums, pieces, top_pieces, cells, pairs,
    lists, wanted, codes, row, lane, tops, slots, near_s, work_s, slot_s,
    load_sem, send_sem, recv_sem, local_sem,
):
    g, s = lax.axis_index("dom"), lax.axis_index("sub")
    core, chip = lax.rem(s, 2), s // 2
    sibling = (g, s + 1 - 2 * core)
    up, down, over = [(g, lax.rem(s + k, SUB)) for k in (2, 6, 4)]
    along = [up, down, over]
    across = [(lax.rem(g + k, DOM), s) for k in range(1, DOM)]
    within = [(g, lax.rem(s + k, SUB)) for k in range(1, SUB)]
    used = [0]

    inputs = [
        pltpu.make_async_copy(a, b, load_sem.at[k])
        for k, (a, b) in enumerate(((pos_in, pos), (vel_in, vel), (acc_in, acc), (act_in, act), (mass_in, mass)))
    ]
    for c in inputs:
        c.start()

    barrier = pltpu.get_barrier_semaphore()
    for peer in across + within:
        pl.semaphore_signal(barrier, inc=1, device_id=peer, device_id_type=MESH)
    pl.semaphore_wait(barrier, DOM + SUB - 2)

    def send(ref, peers, source=None):
        copies = []
        for peer in peers:
            k = used[0]
            used[0] += 1
            copies.append(
                pltpu.make_async_remote_copy(
                    src_ref=ref if source is None else source, dst_ref=ref, send_sem=send_sem.at[k],
                    recv_sem=recv_sem.at[k], device_id=peer, device_id_type=MESH,
                )
            )
            copies[-1].start()
        return copies

    def done(copies):
        for c in copies:
            c.wait()

    below, above, facing = [lax.rem(chip + k, 4) for k in (3, 1, 2)]
    low, high = pl.ds(0, BUCKETS // 2), pl.ds(BUCKETS // 2, BUCKETS // 2)

    def ring_1(buf):
        return send(buf.at[core, chip], [up, down, sibling])

    def ring_2(buf, first):
        first[0].wait_recv()
        found = send(buf.at[core, below, low], [up])
        more = send(buf.at[core, below], [sibling])
        first[1].wait_recv()
        found += send(buf.at[core, above, high], [down])
        more += send(buf.at[core, above], [sibling])
        return found, more

    def ring_3(buf, first, second):
        found, more = second
        for c in found:
            c.wait_recv()
        final = send(buf.at[core, facing], [sibling])
        for c in first + found:
            c.wait_send()
        first[2].wait_recv()
        done(more)
        return final

    list_copies = send(lists.at[core, chip], along, packed)
    for c in inputs:
        c.wait()

    def first(b, carry):
        sl = pl.ds(pl.multiple_of(b * WIDE, WIDE), WIDE)
        a = act[:, sl].astype(f32)
        h = vel[:, sl] + kick * a * acc[:, sl]
        p = pos[:, sl] + time_step * h
        half[:, sl] = h
        m = mass[:, sl]
        x[core, chip, b] = jnp.concatenate([p, m], axis=0)
        ahead[core, chip, b] = jnp.concatenate([p + time_step * h, a], axis=0)
        for c in range(3):
            dense[c, pl.ds(b, 1), :] = p[c : c + 1]
        dense[3, pl.ds(b, 1), :] = m
        return carry

    lax.fori_loop(0, BUCKETS, first, 0, unroll=4)
    x_1 = ring_1(x)
    lists[core, chip] = packed[...]

    def near_part(load, begin, end):
        def item(w, carry):
            pairs[w] = near_item(load, [near_s[w, NEAR_AT + k] for k in range(4)])
            return carry

        lax.fori_loop(begin, end, item, 0, unroll=4)

    def top_sums(table, part):
        base = (s * DOM + g) * 32
        ids = lax.broadcasted_iota(i32, (32, BUCKETS), 0) + base
        sums[...] = jnp.zeros_like(sums)

        def step(i, carry):
            at, k = i // 4, (i % 4) * 4
            got = [top_values(table[at // 4, at % 4, k + u], ids) for u in range(4)]
            v = jnp.concatenate([a for a, _ in got], axis=1)
            o = jnp.concatenate([b for _, b in got], axis=1)
            sums[...] += dot(v, o, (1, 1))
            return carry

        lax.fori_loop(0, SUB * DOM // 4, step, 0, unroll=4)
        mine = top_record(sums[0:16] + sums[16:32] + sums[32:48], base)
        four = jnp.concatenate([mine] * 4, axis=1)
        quarter = lax.broadcasted_iota(i32, (16, 128), 1) // 32
        part[g] = jnp.where(quarter == lax.rem(g, 4), four, 0.0)

    def four_parts(top, part):
        for k in range(4):
            top[s, k] = part[4 * k] + part[4 * k + 1] + part[4 * k + 2] + part[4 * k + 3]

    def essential_cells(table):
        spread(lambda k: table[k // 64, k // 16 % 4, k % 16], pieces, SUB * DOM)

        def gather(i, carry):
            ess = lookup(pieces, SUB * DOM, row[pl.ds(i, 1), :], lane[pl.ds(i, 1), :])
            blank = jnp.zeros((16, 64), f32)
            for u in range(4):
                cells[i * 4 + u] = jnp.concatenate([ess[:, u * 64 : u * 64 + 64], blank], axis=1)
            return carry

        lax.fori_loop(0, ITEMS // 4, gather, 0)

    def top_cells(top):
        spread(lambda k: top[k // 4, k % 4], top_pieces, 32)

        def gather(i, carry):
            t = tops[pl.ds(i, 1), :]
            far = lookup(top_pieces, 32, t >> 7, t & 127)
            blank = [jnp.zeros((16, n), f32) for n in (64, 32)]
            for u in range(8):
                cells[i * 8 + u] += jnp.concatenate([blank[0], far[:, u * 32 : u * 32 + 32], blank[1]], axis=1)
            return carry

        lax.fori_loop(0, ITEMS // 8, gather, 0)

    def far_and_return(load, force):
        def item(w, carry):
            _, origin, y = from_first(load(near_s[w, NEAR_AT]))
            a = pairs[w] + far_item(cells[w], origin, y)
            for c in range(3):
                force[core, chip, c, pl.ds(w, 1), :] = a[c : c + 1]
            return carry

        cuts, flights = (0, 24, ITEMS), []
        for begin, end in zip(cuts, cuts[1:]):
            lax.fori_loop(begin, end, item, 0, unroll=4)
            flights.append(send(force.at[core, chip, :, pl.ds(begin, end - begin), :], along))
        last = []
        for (begin, end), flight in zip(zip(cuts, cuts[1:]), flights):
            done(flight)
            last += send(force.at[core, :, :, pl.ds(begin, end - begin), :], [sibling])
        done(last)

    moments(dense, top_row[...], table_1.at[core, chip, g])
    flight = send(table_1.at[core, chip, g], across)
    done(list_copies)
    list_copies = send(lists.at[core], [sibling])
    done(flight)
    flight = send(table_1.at[core, chip], along)
    done(list_copies)

    def take(w, carry):
        n = work[w]
        wanted[pl.ds(w, 1), :] = lists[(n >> 7) & 1, n >> 8, pl.ds(n & 127, 1), :]
        return carry

    lax.fori_loop(0, ITEMS, take, 0, unroll=4)
    to_scalars = [pltpu.make_async_copy(wanted, near_s, local_sem.at[0])]
    for k in range(SUB):
        to_scalars.append(
            pltpu.make_async_copy(lists.at[k // 4, k % 4, pl.ds(128, 8)], work_s.at[k], local_sem.at[1 + k])
        )
    for c in to_scalars:
        c.start()
    for k in range(SUB):
        codes[4 * k : 4 * k + 4, :] = lists[k % 2, k // 2, 128:132, :]

    def place(i, carry):
        ids = jnp.concatenate([wanted[pl.ds(4 * i + u, 1), :][:, 0:64] for u in range(4)], axis=1)
        hot = jnp.where(row_iota((128, 256)) == (ids & 127), 1.0, 0.0)
        at = row_iota((32, 256)) == (ids >> 7)
        for got, where in ((codes[...] >> 7, row), (codes[...] & 127, lane)):
            found = dot(got.astype(f32), hot, (1, 0))
            where[pl.ds(i, 1), :] = jnp.sum(jnp.where(at, found, 0.0), axis=0, keepdims=True).astype(i32)
        return carry

    lax.fori_loop(0, ITEMS // 4, place, 0)
    for i in range(ITEMS // 8):
        tops[i : i + 1, :] = jnp.concatenate([wanted[8 * i + u : 8 * i + u + 1, 64:96] for u in range(8)], axis=1)
    x_2 = ring_2(x, x_1)
    for c in to_scalars:
        c.wait()
    number = row_iota((SUB, 128)) * 128 + lax.broadcasted_iota(i32, (SUB, 128), 1)

    def find(w, found):
        for k in range(SUB):
            found = jnp.where(number == work_s[k, 4, w], k * ITEMS + w, found)
        return found

    slots[...] = lax.fori_loop(0, ITEMS, find, jnp.full((SUB, 128), -1, i32))
    slot_copy = pltpu.make_async_copy(slots, slot_s, local_sem.at[9])
    slot_copy.start()

    done(flight)
    flight = send(table_1.at[core], [sibling])
    x_3 = ring_3(x, x_1, x_2)
    done(flight)
    top_sums(table_1, part_1)
    flight = send(part_1.at[g], across)
    essential_cells(table_1)
    done(x_3)
    ahead_1 = ring_1(ahead)
    done(flight)
    four_parts(top_1, part_1)
    flight = send(top_1.at[s], within)

    def load_1(n):
        return x[(n >> 7) & 1, n >> 8, n & 127]

    near_part(load_1, 0, 24)
    ahead_2 = ring_2(ahead, ahead_1)
    near_part(load_1, 24, ITEMS)
    done(flight)
    top_cells(top_1)
    ahead_3 = ring_3(ahead, ahead_1, ahead_2)
    far_and_return(load_1, force_1)
    slot_copy.wait()

    def second(b, carry):
        sl = pl.ds(pl.multiple_of(b * WIDE, WIDE), WIDE)
        push = kick * act[:, sl].astype(f32) * forced(force_1, slot_s[s, b])
        h = half[:, sl] + push + push
        p = x[core, chip, b][0:3] + time_step * h
        half[:, sl] = h
        pos_out[:, sl] = p
        for c in range(3):
            dense[c, pl.ds(b, 1), :] = p[c : c + 1]
        return carry

    lax.fori_loop(0, BUCKETS, second, 0, unroll=4)
    moments(dense, top_row[...], table_2.at[core, chip, g])
    flight = send(table_2.at[core, chip, g], across)
    done(ahead_3)

    def load_2(n):
        at = ((n >> 7) & 1, n >> 8, n & 127)
        p = ahead[at]
        moved = p[0:3] + (2.0 * kick * time_step) * p[3:4] * forced(force_1, slot_s[n >> 7, n & 127])
        return jnp.concatenate([moved, x[at][3:4]], axis=0)

    near_part(load_2, 0, 8)
    done(flight)
    flight = send(table_2.at[core, chip], along)
    near_part(load_2, 8, 24)
    done(flight)
    flight = send(table_2.at[core], [sibling])
    near_part(load_2, 24, 32)
    done(flight)
    top_sums(table_2, part_2)
    flight = send(part_2.at[g], across)
    near_part(load_2, 32, ITEMS)
    done(flight)
    four_parts(top_2, part_2)
    flight = send(top_2.at[s], within)
    essential_cells(table_2)
    done(flight)
    top_cells(top_2)
    far_and_return(load_2, force_2)

    def last(b, carry):
        sl = pl.ds(pl.multiple_of(b * WIDE, WIDE), WIDE)
        vel_out[:, sl] = half[:, sl] + kick * act[:, sl].astype(f32) * forced(force_2, slot_s[s, b])
        return carry

    lax.fori_loop(0, BUCKETS, last, 0, unroll=4)


def by_core(s):
    return (s & 1) * (SUB // 2) + (s >> 1)


def body(positions, velocities, masses, accel_prev, active, bucket_top, near_list, cell_list, top_list, essential, work):
    n = positions.shape[1]
    wanted = essential.reshape(DOM, -1)
    codes = (by_core(wanted >> 7) * DOM + jnp.arange(DOM, dtype=i32)[:, None]) * 128 + (wanted & 127)
    lists = jnp.concatenate([cell_list, top_list, near_list, jnp.zeros((BUCKETS, 28), i32)], axis=1)
    tail = jnp.concatenate([work, jnp.full((128 - ITEMS,), -1, i32)])[None]
    packed = jnp.concatenate([lists, codes.reshape(4, 128), tail, jnp.zeros((3, 128), i32)], axis=0)

    vm, dma = pltpu.VMEM, pltpu.SemaphoreType.DMA
    flat = vm((3, n), f32)
    group = vm((2, SUB // 2, BUCKETS, 4, WIDE), f32)
    twice = [
        vm((2, SUB // 2, DOM, 16, 128), f32), vm((SUB, 4, 16, 128), f32), vm((DOM, 16, 128), f32),
        vm((2, SUB // 2, 3, ITEMS, WIDE), f32),
    ]
    scratch = [flat, flat, flat, vm((1, n), i32), vm((1, n), f32), flat, vm((4, BUCKETS, WIDE), f32), group, group]
    scratch += twice + twice
    scratch += [
        vm((48, 32), f32), vm((SUB * DOM * 16, 256), bf16), vm((32 * 16, 256), bf16),
        vm((ITEMS, 16, 128), f32), vm((ITEMS, 4, WIDE), f32),
        vm((2, SUB // 2, BUCKETS + 8, 128), i32), vm((ITEMS, 128), i32), vm((32, 128), i32),
        vm((16, 256), i32), vm((16, 256), i32), vm((8, 256), i32), vm((SUB, 128), i32),
        pltpu.SMEM((ITEMS, 128), i32), pltpu.SMEM((SUB, 8, 128), i32), pltpu.SMEM((SUB, 128), i32),
        dma((5,)), dma((COPIES,)), dma((COPIES,)), dma((10,)),
    ]
    place = lambda where: pl.BlockSpec(memory_space=where)
    shape = jax.ShapeDtypeStruct((3, n), f32)
    return pl.pallas_call(
        kernel,
        out_shape=(shape, shape),
        in_specs=[place(pltpu.SMEM)] + [place(pltpu.HBM)] * 5 + [place(pltpu.VMEM)] * 2,
        out_specs=(place(pltpu.VMEM), place(pltpu.VMEM)),
        scratch_shapes=scratch,
        compiler_params=pltpu.CompilerParams(collective_id=1, has_side_effects=True, vmem_limit_bytes=50 * MIB),
    )(
        work, positions, velocities, accel_prev, active.reshape(1, n), masses.reshape(1, n),
        bucket_top.astype(f32).reshape(1, BUCKETS), packed,
    )


def solution(mesh):
    both = ("dom", "sub")
    in_specs = (
        P(None, both), P(None, both), P(both), P(None, both), P(both), P(both),
        P(both, None), P(both, None), P(both, None), P("dom", "sub", None, None), P(both),
    )
    return jax.shard_map(
        body, mesh=mesh, in_specs=in_specs, out_specs=(P(None, both), P(None, both)), check_vma=False
    )
```

```python
import functools

import jax
import jax.numpy as jnp
from jax import lax
from jax.experimental import pallas as pl
from jax.experimental.pallas import tpu as pltpu
from jax.sharding import PartitionSpec as P

f32, bf16, i32 = jnp.float32, jnp.bfloat16, jnp.int32
MESH = pl.DeviceIdType.MESH
SUB, DOM = 8, 16
BUCKETS, WIDE, ITEMS = 128, 256, 40
GROUP = SUB * BUCKETS
TOP_SIDE = 16
MIB = 2**20

time_step = 0.01
soften = 0.0025
mass_floor = 0.5
kick = 0.5 * time_step
PAIRS = ((0, 0), (1, 1), (2, 2), (0, 1), (0, 2), (1, 2))
NEAR_AT = 96
COPIES = 160


def rnd(a):
    return a.astype(bf16).astype(f32)


def split3(a):
    h = rnd(a)
    r = a - h
    m = rnd(r)
    return h, m, rnd(r - m)


def dot(a, b, dims):
    return lax.dot_general(
        a.astype(bf16), b.astype(bf16), ((dims[:1], dims[1:]), ((), ())), preferred_element_type=f32
    )


def row_iota(shape):
    return lax.broadcasted_iota(i32, shape, 0)


def pick(rows, shape):
    at = row_iota(shape)
    out = jnp.zeros(shape, f32)
    for i, v in rows.items():
        out = jnp.where(at == i, v, out)
    return out


def square(y):
    q = y * y
    return q[0:1] + q[1:2] + q[2:3]


def moments(dense, top_row, rec_ref):
    first = [dense[c][:, 0:1] for c in range(3)]
    y = [dense[c] - first[c] for c in range(3)]
    m = dense[3]
    ones = jnp.ones((8, WIDE), f32)
    lead = jnp.where(lax.broadcasted_iota(i32, (8, WIDE), 1) == 0, 1.0, 0.0)

    def total(a, by=ones):
        return lax.dot_general(
            by, a, (((1,), (1,)), ((), ())), precision=lax.Precision.HIGHEST, preferred_element_type=f32
        )[0:1]

    my = [m * y[c] for c in range(3)]
    mass = total(m)
    start = [total(dense[c], lead) for c in range(3)]
    s = [total(my[c]) for c in range(3)]
    d = [s[c] / mass for c in range(3)]
    second = [total(my[a] * y[b]) - s[a] * d[b] for a, b in PAIRS]
    rows = {0: mass, 10: top_row}
    for c in range(3):
        rows[1 + c] = start[c] + d[c]
    for k in range(6):
        rows[4 + k] = second[k]
    rec_ref[...] = pick(rows, (16, BUCKETS))


def centre(ids):
    return [
        (part.astype(f32) + 0.5) / TOP_SIDE
        for part in (ids >> 8, (ids >> 4) & 15, ids & 15)
    ]


def spread(table, pieces, rows):
    at = row_iota((16, 128))
    extra = (at >= 11) & (at < 14)

    def step(k, carry):
        t = table(k)
        h, m, l = split3(t)
        low = pltpu.roll(l, 10, 0)
        both = jnp.concatenate([jnp.where(extra, low, h), jnp.where(extra, 0.0, m)], axis=1)
        pieces[pl.ds(pl.multiple_of(k * 16, 16), 16), :] = both.astype(bf16)
        return carry

    lax.fori_loop(0, rows, step, 0, unroll=4)


def lookup(pieces, rows, row, lane):
    n = row.shape[1]
    hot = jnp.where(row_iota((128, n)) == lane, 1.0, 0.0).astype(bf16)
    hot = jnp.concatenate([hot, hot], axis=0)
    row16 = jnp.broadcast_to(row, (16, n))

    def step(i, got):
        block = pieces[pl.ds(pl.multiple_of(i * 128, 128), 128), :]
        found = dot(block, hot, (1, 0))
        for u in range(8):
            got = jnp.where(row16 == i * 8 + u, found[u * 16 : u * 16 + 16], got)
        return got

    return lax.fori_loop(0, rows // 8, step, jnp.zeros((16, n), f32), unroll=rows // 8)


def from_first(first):
    is_pos = row_iota((4, WIDE)) < 3
    origin = jnp.where(is_pos, jnp.broadcast_to(first[:, 0:1], (4, WIDE)), 0.0)
    return is_pos, origin, first - origin


def near_item(load, ids):
    first = load(ids[0])
    is_pos, origin, y = from_first(first)
    h = rnd(y)
    mid = rnd(y - h)
    fine = h + mid
    th, tm, tl = split3(square(fine))
    far_h = jnp.where(is_pos, -2.0 * h, 0.0)
    far_m = jnp.where(is_pos, -2.0 * mid, 0.0)
    one = jnp.ones((1, WIDE), f32)
    ct = pick({0: one, 1: one, 2: one, 3: th, 4: tm, 5: tl}, (8, WIDE))
    target = jnp.concatenate([far_h, far_h, far_m, far_m, ct], axis=0).astype(bf16)
    total = jnp.zeros((WIDE, 16), f32)
    for k in range(4):
        raw = first if k == 0 else load(ids[k])
        ys = raw - origin
        sh = rnd(ys)
        sm = rnd(ys - sh)
        sf = sh + sm
        qh, qm, ql = split3(square(sf) + soften)
        cs = pick({0: qh, 1: qm, 2: ql, 3: one, 4: one, 5: one}, (8, WIDE))
        source = jnp.concatenate([sh, sm, sh, sm, cs], axis=0)
        r = lax.rsqrt(dot(target, source, (0, 0)))
        w = (r * r * r).astype(bf16)
        z = jnp.where(is_pos, sf * raw[3:4], raw)
        zh, zm, zl = split3(z)
        left = jnp.concatenate([zh, zm, zl, jnp.zeros((4, WIDE), f32)], axis=0)
        total = total + dot(w, left, (1, 1))
    total = total.T
    s = total[0:4] + total[4:8] + total[8:12]
    return s - fine * s[3:4]


def far_item(cells, origin, y):
    o = [jnp.broadcast_to(origin[i : i + 1, 0:1], (1, 128)) for i in range(3)]
    mass = cells[0:1]
    px, py, pz = [cells[1 + c : 2 + c] + cells[11 + c : 12 + c] - o[c] for c in range(3)]
    trace = cells[4:5] + cells[5:6] + cells[6:7]
    qxx, qyy, qzz = [3.0 * cells[i : i + 1] - trace for i in (4, 5, 6)]
    qxy, qxz, qyz = [3.0 * cells[i : i + 1] for i in (7, 8, 9)]
    gx = qxx * px + qxy * py + qxz * pz
    gy = qxy * px + qyy * py + qyz * pz
    gz = qxz * px + qyz * py + qzz * pz
    one = jnp.ones((1, 128), f32)
    pp = px * px + py * py + pz * pz + soften
    cs = pick({0: pp, 1: -2.0 * px, 2: -2.0 * py, 3: -2.0 * pz, 4: one, 5: one, 6: one}, (16, 128))
    pg = px * gx + py * gy + pz * gz
    cq = pick(
        {0: pg, 1: -2.0 * gx, 2: -2.0 * gy, 3: -2.0 * gz, 4: qxx, 5: qyy, 6: qzz, 7: 2.0 * qxy, 8: 2.0 * qxz, 9: 2.0 * qyz},
        (16, 128),
    )
    c = jnp.concatenate([cs, cq], axis=1)
    a, b, d = y[0:1], y[1:2], y[2:3]
    ones = jnp.ones((1, WIDE), f32)
    phi = pick(
        {0: ones, 1: a, 2: b, 3: d, 4: a * a, 5: b * b, 6: d * d, 7: a * b, 8: a * d, 9: b * d}, (16, WIDE)
    )
    ch, cm, cl = split3(c)
    fh, fm, fl = split3(phi)
    sq = dot(
        jnp.concatenate([ch, ch, cm, cm, ch, cl], axis=0),
        jnp.concatenate([fh, fm, fh, fm, fl, fh], axis=0),
        (0, 0),
    )
    s, q = sq[0:128], sq[128:256]
    r = lax.rsqrt(s)
    r2 = r * r
    r3 = r * r2
    r5 = r3 * r2
    l1 = pick({0: mass * px, 1: mass * py, 2: mass * pz, 3: -mass}, (16, 128))
    l2 = pick({0: 2.5 * px, 1: 2.5 * py, 2: 2.5 * pz, 3: -2.5 * one}, (16, 128))
    l3 = pick({0: -gx, 1: -gy, 2: -gz, 4: qxx, 5: qyy, 6: qzz, 7: qxy, 8: qxz, 9: qyz}, (16, 128))
    out = jnp.zeros((32, WIDE), f32)
    for l, v in ((l1, r3), (l2, q * (r5 * r2)), (l3, r5)):
        lh = rnd(l)
        pieces = jnp.concatenate([lh, rnd(l - lh)], axis=0)
        vh = v.astype(bf16)
        vm = (v - vh.astype(f32)).astype(bf16)
        out = out + dot(
            jnp.concatenate([pieces, pieces], axis=1), jnp.concatenate([vh, vm], axis=0), (1, 0)
        )
    t = out[0:16] + out[16:32]
    axx, ayy, azz, axy, axz, ayz = [t[i : i + 1] for i in range(4, 10)]
    turned = pick(
        {0: axx * a + axy * b + axz * d, 1: axy * a + ayy * b + ayz * d, 2: axz * a + ayz * b + azz * d}, (4, WIDE)
    )
    return t[0:4] + t[3:4] * y + turned


def top_values(t, ids):
    mass = t[0:1]
    own = t[10:11].astype(i32)
    d = [t[1 + c : 2 + c] - at for c, at in enumerate(centre(own))]
    md = [mass * d[c] for c in range(3)]
    rows = {0: mass, 1: md[0], 2: md[1], 3: md[2]}
    for k, (a, b) in enumerate(PAIRS):
        rows[4 + k] = t[4 + k : 5 + k] + md[a] * d[b]
    pieces = jnp.concatenate(split3(pick(rows, (16, BUCKETS))), axis=0)
    return pieces, jnp.where(ids == own, 1.0, 0.0)


def top_record(t, base):
    mass = t[0:1]
    w = jnp.maximum(mass, mass_floor)
    at = centre(lax.broadcasted_iota(i32, (1, 32), 1) + base)
    u = [t[1 + c : 2 + c] / w for c in range(3)]
    rows = {0: mass}
    for c in range(3):
        rows[1 + c] = at[c] + u[c]
    for k, (a, b) in enumerate(PAIRS):
        rows[4 + k] = t[4 + k : 5 + k] - t[1 + a : 2 + a] * u[b]
    return pick(rows, (16, 32))


def by_core(s):
    return (s & 1) * (SUB // 2) + (s >> 1)


def forced(force, slot):
    k = jnp.maximum(slot, 0)
    block, w = k // ITEMS, lax.rem(k, ITEMS)
    rows = [force[block // 4, lax.rem(block, 4), c, pl.ds(w, 1), :] for c in range(3)]
    return jnp.where(slot >= 0, jnp.concatenate(rows, axis=0), 0.0)


def kernel(
    work, pos_in, vel_in, acc_in, act_in, mass_in, top_row, cell_list, top_list, near_list, requests, work_row,
    vel_out, pos_out,
    pos, vel, acc, act, mass, half, dense, x, ahead,
    table_1, top_1, part_1, force_1, table_2, top_2, part_2, force_2,
    sums, pieces, top_pieces, cells, pairs,
    lists, wanted, codes, row, lane, tops, slots, near_s, work_s, slot_s,
    load_sem, send_sem, recv_sem, local_sem,
):
    g, s = lax.axis_index("dom"), lax.axis_index("sub")
    core, chip = lax.rem(s, 2), s // 2
    sibling = (g, s + 1 - 2 * core)
    up, down, over = [(g, lax.rem(s + k, SUB)) for k in (2, 6, 4)]
    along = [up, down, over]
    across = [(lax.rem(g + k, DOM), s) for k in range(1, DOM)]
    within = [(g, lax.rem(s + k, SUB)) for k in range(1, SUB)]
    used = [0]

    inputs = [
        pltpu.make_async_copy(a, b, load_sem.at[k])
        for k, (a, b) in enumerate(((pos_in, pos), (vel_in, vel), (acc_in, acc), (act_in, act), (mass_in, mass)))
    ]
    for c in inputs:
        c.start()

    barrier = pltpu.get_barrier_semaphore()
    for peer in across + within:
        pl.semaphore_signal(barrier, inc=1, device_id=peer, device_id_type=MESH)
    def send(ref, peers, source=None):
        copies = []
        for peer in peers:
            k = used[0]
            used[0] += 1
            copies.append(
                pltpu.make_async_remote_copy(
                    src_ref=ref if source is None else source, dst_ref=ref, send_sem=send_sem.at[k],
                    recv_sem=recv_sem.at[k], device_id=peer, device_id_type=MESH,
                )
            )
            copies[-1].start()
        return copies

    def done(copies):
        for c in copies:
            c.wait()

    below, above, facing = [lax.rem(chip + k, 4) for k in (3, 1, 2)]
    low, high = pl.ds(0, BUCKETS // 2), pl.ds(BUCKETS // 2, BUCKETS // 2)

    def ring_1(buf):
        return send(buf.at[core, chip], [up, down, sibling])

    def ring_2(buf, first):
        first[0].wait_recv()
        found = send(buf.at[core, below, low], [up])
        more = send(buf.at[core, below], [sibling])
        first[1].wait_recv()
        found += send(buf.at[core, above, high], [down])
        more += send(buf.at[core, above], [sibling])
        return found, more

    def ring_3(buf, first, second):
        found, more = second
        for c in found:
            c.wait_recv()
        final = send(buf.at[core, facing], [sibling])
        for c in first + found:
            c.wait_send()
        first[2].wait_recv()
        done(more)
        return final

    for c in inputs:
        c.wait()

    def first(b, carry):
        sl = pl.ds(pl.multiple_of(b * WIDE, WIDE), WIDE)
        a = act[:, sl].astype(f32)
        h = vel[:, sl] + kick * a * acc[:, sl]
        p = pos[:, sl] + time_step * h
        half[:, sl] = h
        m = mass[:, sl]
        x[core, chip, b] = jnp.concatenate([p, m], axis=0)
        ahead[core, chip, b] = jnp.concatenate([p + time_step * h, a], axis=0)
        for c in range(3):
            dense[c, pl.ds(b, 1), :] = p[c : c + 1]
        dense[3, pl.ds(b, 1), :] = m
        return carry

    lax.fori_loop(0, BUCKETS, first, 0, unroll=4)
    pl.semaphore_wait(barrier, DOM + SUB - 2)
    x_1 = ring_1(x)
    turned = [cell_list[...], top_list[...], near_list[...], jnp.zeros((28, BUCKETS), i32)]
    lists[core, chip, 0:BUCKETS, :] = jnp.concatenate(turned, axis=0).T
    asked = requests[...]
    asked = (by_core(asked >> 7) * DOM + row_iota((DOM, 32))) * 128 + (asked & 127)
    rest = [jnp.concatenate([asked[4 * r + k : 4 * r + k + 1] for k in range(4)], axis=1) for r in range(4)]
    rest.append(jnp.concatenate([work_row[...], jnp.full((1, 128 - ITEMS), -1, i32)], axis=1))
    lists[core, chip, BUCKETS : BUCKETS + 8, :] = jnp.concatenate(rest + [jnp.zeros((3, 128), i32)], axis=0)
    list_copies = send(lists.at[core, chip], along)

    def near_part(load, begin, end):
        def item(w, carry):
            pairs[w] = near_item(load, [near_s[w, NEAR_AT + k] for k in range(4)])
            return carry

        lax.fori_loop(begin, end, item, 0, unroll=4)

    def top_sums(table, part):
        base = (s * DOM + g) * 32
        ids = lax.broadcasted_iota(i32, (32, BUCKETS), 0) + base
        sums[...] = jnp.zeros_like(sums)

        def step(i, carry):
            at, k = i // 4, (i % 4) * 4
            got = [top_values(table[at // 4, at % 4, k + u], ids) for u in range(4)]
            v = jnp.concatenate([a for a, _ in got], axis=1)
            o = jnp.concatenate([b for _, b in got], axis=1)
            sums[...] += dot(v, o, (1, 1))
            return carry

        lax.fori_loop(0, SUB * DOM // 4, step, 0, unroll=4)
        mine = top_record(sums[0:16] + sums[16:32] + sums[32:48], base)
        four = jnp.concatenate([mine] * 4, axis=1)
        quarter = lax.broadcasted_iota(i32, (16, 128), 1) // 32
        part[g] = jnp.where(quarter == lax.rem(g, 4), four, 0.0)

    def four_parts(top, part):
        for k in range(4):
            top[s, k] = part[4 * k] + part[4 * k + 1] + part[4 * k + 2] + part[4 * k + 3]

    def essential_cells(table):
        spread(lambda k: table[k // 64, k // 16 % 4, k % 16], pieces, SUB * DOM)

        def gather(i, carry):
            ess = lookup(pieces, SUB * DOM, row[pl.ds(i, 1), :], lane[pl.ds(i, 1), :])
            blank = jnp.zeros((16, 64), f32)
            for u in range(4):
                cells[i * 4 + u] = jnp.concatenate([ess[:, u * 64 : u * 64 + 64], blank], axis=1)
            return carry

        lax.fori_loop(0, ITEMS // 4, gather, 0)

    def top_cells(top):
        spread(lambda k: top[k // 4, k % 4], top_pieces, 32)

        def gather(i, carry):
            t = tops[pl.ds(i, 1), :]
            far = lookup(top_pieces, 32, t >> 7, t & 127)
            blank = [jnp.zeros((16, n), f32) for n in (64, 32)]
            for u in range(8):
                cells[i * 8 + u] += jnp.concatenate([blank[0], far[:, u * 32 : u * 32 + 32], blank[1]], axis=1)
            return carry

        lax.fori_loop(0, ITEMS // 8, gather, 0)

    def finish(load, force, known):
        first_sem = used[0]
        used[0] += 16

        def copy(ref, k, peer):
            return pltpu.make_async_remote_copy(
                src_ref=ref, dst_ref=ref, send_sem=send_sem.at[k], recv_sem=recv_sem.at[k],
                device_id=peer, device_id_type=MESH,
            )

        def rows(p):
            return pl.ds(pl.multiple_of(p * 8, 8), 8)

        def by_links(p):
            ref = force.at[core, chip, :, rows(p), :]
            return [copy(ref, first_sem + p * 3 + k, peer) for k, peer in enumerate(along)]

        def to_sibling(p):
            return copy(force.at[core, :, :, rows(p), :], first_sem + 12 + p, sibling)

        def forward(p):
            done(by_links(p))
            to_sibling(p).start()

        def compute(p, with_near):
            def item(i, carry):
                w = p * 8 + i
                _, origin, y = from_first(load(near_s[w, NEAR_AT]))
                if with_near:
                    a = near_item(load, [near_s[w, NEAR_AT + k] for k in range(4)])
                else:
                    a = pairs[w]
                a = a + far_item(cells[w], origin, y)
                for c in range(3):
                    force[core, chip, c, pl.ds(w, 1), :] = a[c : c + 1]
                return carry

            lax.fori_loop(0, 8, item, 0, unroll=4)

        def piece(p, carry, with_near):
            compute(p, with_near)
            for c in by_links(p):
                c.start()

            @pl.when(p > 0)
            def _():
                forward(p - 1)

            return carry

        if known:
            lax.fori_loop(0, known // 8, functools.partial(piece, with_near=False), 0)
        lax.fori_loop(known // 8, 4, functools.partial(piece, with_near=True), 0)
        compute(4, True)
        final = send(force.at[core, chip, :, pl.ds(32, 8), :], within)
        forward(3)
        done(final)
        for p in range(4):
            to_sibling(p).wait()

    moments(dense, top_row[...].astype(f32), table_1.at[core, chip, g])
    flight = send(table_1.at[core, chip, g], across)
    done(list_copies)
    list_copies = send(lists.at[core], [sibling])
    done(flight)
    flight = send(table_1.at[core, chip], along)
    x_2 = ring_2(x, x_1)
    done(list_copies)

    def take(w, carry):
        n = work[w]
        wanted[pl.ds(w, 1), :] = lists[(n >> 7) & 1, n >> 8, pl.ds(n & 127, 1), :]
        return carry

    lax.fori_loop(0, ITEMS, take, 0, unroll=4)
    to_scalars = [pltpu.make_async_copy(wanted, near_s, local_sem.at[0])]
    for k in range(SUB):
        to_scalars.append(
            pltpu.make_async_copy(lists.at[k // 4, k % 4, pl.ds(128, 8)], work_s.at[k], local_sem.at[1 + k])
        )
    for c in to_scalars:
        c.start()
    for k in range(SUB):
        codes[4 * k : 4 * k + 4, :] = lists[k % 2, k // 2, 128:132, :]

    def place(i, carry):
        ids = jnp.concatenate([wanted[pl.ds(4 * i + u, 1), :][:, 0:64] for u in range(4)], axis=1)
        hot = jnp.where(row_iota((128, 256)) == (ids & 127), 1.0, 0.0)
        at = row_iota((32, 256)) == (ids >> 7)
        for got, where in ((codes[...] >> 7, row), (codes[...] & 127, lane)):
            found = dot(got.astype(f32), hot, (1, 0))
            where[pl.ds(i, 1), :] = jnp.sum(jnp.where(at, found, 0.0), axis=0, keepdims=True).astype(i32)
        return carry

    lax.fori_loop(0, ITEMS // 4, place, 0)
    for i in range(ITEMS // 8):
        tops[i : i + 1, :] = jnp.concatenate([wanted[8 * i + u : 8 * i + u + 1, 64:96] for u in range(8)], axis=1)
    for c in to_scalars:
        c.wait()
    number = row_iota((SUB, 128)) * 128 + lax.broadcasted_iota(i32, (SUB, 128), 1)

    def find(w, found):
        for k in range(SUB):
            found = jnp.where(number == work_s[k, 4, w], k * ITEMS + w, found)
        return found

    slots[...] = lax.fori_loop(0, ITEMS, find, jnp.full((SUB, 128), -1, i32))
    slot_copy = pltpu.make_async_copy(slots, slot_s, local_sem.at[9])
    slot_copy.start()

    done(flight)
    flight = send(table_1.at[core], [sibling])
    done(flight)
    top_sums(table_1, part_1)
    flight = send(part_1.at[g], across)
    x_3 = ring_3(x, x_1, x_2)
    essential_cells(table_1)
    done(flight)
    four_parts(top_1, part_1)
    flight = send(top_1.at[s], within)
    done(x_3)
    ahead_1 = ring_1(ahead)
    done(flight)
    top_cells(top_1)

    def load_1(n):
        return x[(n >> 7) & 1, n >> 8, n & 127]

    finish(load_1, force_1, 0)
    ahead_2 = ring_2(ahead, ahead_1)
    slot_copy.wait()

    def second(b, carry):
        sl = pl.ds(pl.multiple_of(b * WIDE, WIDE), WIDE)
        push = kick * act[:, sl].astype(f32) * forced(force_1, slot_s[s, b])
        h = half[:, sl] + push + push
        p = x[core, chip, b][0:3] + time_step * h
        half[:, sl] = h
        pos_out[:, sl] = p
        for c in range(3):
            dense[c, pl.ds(b, 1), :] = p[c : c + 1]
        return carry

    lax.fori_loop(0, BUCKETS, second, 0, unroll=4)
    moments(dense, top_row[...].astype(f32), table_2.at[core, chip, g])
    flight = send(table_2.at[core, chip, g], across)
    ahead_3 = ring_3(ahead, ahead_1, ahead_2)
    done(ahead_3)

    def load_2(n):
        at = ((n >> 7) & 1, n >> 8, n & 127)
        p = ahead[at]
        moved = p[0:3] + (2.0 * kick * time_step) * p[3:4] * forced(force_1, slot_s[n >> 7, n & 127])
        return jnp.concatenate([moved, x[at][3:4]], axis=0)

    near_part(load_2, 0, 4)
    done(flight)
    flight = send(table_2.at[core, chip], along)
    near_part(load_2, 4, 16)
    done(flight)
    flight = send(table_2.at[core], [sibling])
    near_part(load_2, 16, 20)
    done(flight)
    top_sums(table_2, part_2)
    flight = send(part_2.at[g], across)
    essential_cells(table_2)
    done(flight)
    four_parts(top_2, part_2)
    flight = send(top_2.at[s], within)
    near_part(load_2, 20, 24)
    done(flight)
    top_cells(top_2)
    finish(load_2, force_2, 24)

    def last(b, carry):
        sl = pl.ds(pl.multiple_of(b * WIDE, WIDE), WIDE)
        vel_out[:, sl] = half[:, sl] + kick * act[:, sl].astype(f32) * forced(force_2, slot_s[s, b])
        return carry

    lax.fori_loop(0, BUCKETS, last, 0, unroll=4)


def body(positions, velocities, masses, accel_prev, active, bucket_top, near_list, cell_list, top_list, essential, work):
    n = positions.shape[1]
    vm, dma = pltpu.VMEM, pltpu.SemaphoreType.DMA
    flat = vm((3, n), f32)
    group = vm((2, SUB // 2, BUCKETS, 4, WIDE), f32)
    twice = [
        vm((2, SUB // 2, DOM, 16, 128), f32), vm((SUB, 4, 16, 128), f32), vm((DOM, 16, 128), f32),
        vm((2, SUB // 2, 3, ITEMS, WIDE), f32),
    ]
    scratch = [flat, flat, flat, vm((1, n), i32), vm((1, n), f32), flat, vm((4, BUCKETS, WIDE), f32), group, group]
    scratch += twice + twice
    scratch += [
        vm((48, 32), f32), vm((SUB * DOM * 16, 256), bf16), vm((32 * 16, 256), bf16),
        vm((ITEMS, 16, 128), f32), vm((ITEMS, 4, WIDE), f32),
        vm((2, SUB // 2, BUCKETS + 8, 128), i32), vm((ITEMS, 128), i32), vm((32, 128), i32),
        vm((16, 256), i32), vm((16, 256), i32), vm((8, 256), i32), vm((SUB, 128), i32),
        pltpu.SMEM((ITEMS, 128), i32), pltpu.SMEM((SUB, 8, 128), i32), pltpu.SMEM((SUB, 128), i32),
        dma((5,)), dma((COPIES,)), dma((COPIES,)), dma((10,)),
    ]
    place = lambda where: pl.BlockSpec(memory_space=where)
    shape = jax.ShapeDtypeStruct((3, n), f32)
    return pl.pallas_call(
        kernel,
        out_shape=(shape, shape),
        in_specs=[place(pltpu.SMEM)] + [place(pltpu.HBM)] * 5 + [place(pltpu.VMEM)] * 6,
        out_specs=(place(pltpu.VMEM), place(pltpu.VMEM)),
        scratch_shapes=scratch,
        compiler_params=pltpu.CompilerParams(collective_id=1, has_side_effects=True, vmem_limit_bytes=62 * MIB),
    )(
        work, positions, velocities, accel_prev, active.reshape(1, n), masses.reshape(1, n),
        bucket_top.reshape(1, BUCKETS), cell_list.T, top_list.T, near_list.T, essential.reshape(DOM, -1),
        work.reshape(1, ITEMS),
    )


def solution(mesh):
    both = ("dom", "sub")
    in_specs = (
        P(None, both), P(None, both), P(both), P(None, both), P(both), P(both),
        P(both, None), P(both, None), P(both, None), P("dom", "sub", None, None), P(both),
    )
    return jax.shard_map(
        body, mesh=mesh, in_specs=in_specs, out_specs=(P(None, both), P(None, both)), check_vma=False
    )
```

```python
import functools

import jax
import jax.numpy as jnp
from jax import lax
from jax.experimental import pallas as pl
from jax.experimental.pallas import tpu as pltpu
from jax.sharding import PartitionSpec as P

f32, bf16, i32 = jnp.float32, jnp.bfloat16, jnp.int32
MESH = pl.DeviceIdType.MESH
SUB, DOM = 8, 16
BUCKETS, WIDE, ITEMS = 128, 256, 40
GROUP = SUB * BUCKETS
TOP_SIDE = 16
MIB = 2**20

time_step = 0.01
soften = 0.0025
mass_floor = 0.5
kick = 0.5 * time_step
PAIRS = ((0, 0), (1, 1), (2, 2), (0, 1), (0, 2), (1, 2))
NEAR_AT = 96
COPIES = 160


def rnd(a):
    return a.astype(bf16).astype(f32)


def split3(a):
    h = rnd(a)
    r = a - h
    m = rnd(r)
    return h, m, rnd(r - m)


def dot(a, b, dims):
    return lax.dot_general(
        a.astype(bf16), b.astype(bf16), ((dims[:1], dims[1:]), ((), ())), preferred_element_type=f32
    )


def row_iota(shape):
    return lax.broadcasted_iota(i32, shape, 0)


def pick(rows, shape):
    at = row_iota(shape)
    out = jnp.zeros(shape, f32)
    for i, v in rows.items():
        out = jnp.where(at == i, v, out)
    return out


def square(y):
    q = y * y
    return q[0:1] + q[1:2] + q[2:3]


def moments(dense, top_row, rec_ref):
    first = [dense[c][:, 0:1] for c in range(3)]
    y = [dense[c] - first[c] for c in range(3)]
    m = dense[3]
    ones = jnp.ones((8, WIDE), f32)
    lead = jnp.where(lax.broadcasted_iota(i32, (8, WIDE), 1) == 0, 1.0, 0.0)

    def total(a, by=ones):
        return lax.dot_general(
            by, a, (((1,), (1,)), ((), ())), precision=lax.Precision.HIGHEST, preferred_element_type=f32
        )[0:1]

    my = [m * y[c] for c in range(3)]
    mass = total(m)
    start = [total(dense[c], lead) for c in range(3)]
    s = [total(my[c]) for c in range(3)]
    d = [s[c] / mass for c in range(3)]
    second = [total(my[a] * y[b]) - s[a] * d[b] for a, b in PAIRS]
    rows = {0: mass, 10: top_row}
    for c in range(3):
        rows[1 + c] = start[c] + d[c]
    for k in range(6):
        rows[4 + k] = second[k]
    rec_ref[...] = pick(rows, (16, BUCKETS))


def centre(ids):
    return [
        (part.astype(f32) + 0.5) / TOP_SIDE
        for part in (ids >> 8, (ids >> 4) & 15, ids & 15)
    ]


def spread(table, pieces, rows):
    at = row_iota((16, 128))
    extra = (at >= 11) & (at < 14)

    def step(k, carry):
        t = table(k)
        h, m, l = split3(t)
        low = pltpu.roll(l, 10, 0)
        both = jnp.concatenate([jnp.where(extra, low, h), jnp.where(extra, 0.0, m)], axis=1)
        pieces[pl.ds(pl.multiple_of(k * 16, 16), 16), :] = both.astype(bf16)
        return carry

    lax.fori_loop(0, rows, step, 0, unroll=4)


def lookup(pieces, rows, row, lane):
    n = row.shape[1]
    hot = jnp.where(row_iota((128, n)) == lane, 1.0, 0.0).astype(bf16)
    hot = jnp.concatenate([hot, hot], axis=0)
    row16 = jnp.broadcast_to(row, (16, n))

    def step(i, got):
        block = pieces[pl.ds(pl.multiple_of(i * 128, 128), 128), :]
        found = dot(block, hot, (1, 0))
        for u in range(8):
            got = jnp.where(row16 == i * 8 + u, found[u * 16 : u * 16 + 16], got)
        return got

    return lax.fori_loop(0, rows // 8, step, jnp.zeros((16, n), f32), unroll=rows // 8)


def from_first(first):
    is_pos = row_iota((4, WIDE)) < 3
    origin = jnp.where(is_pos, jnp.broadcast_to(first[:, 0:1], (4, WIDE)), 0.0)
    return is_pos, origin, first - origin


def near_item(load, ids):
    first = load(ids[0])
    is_pos, origin, y = from_first(first)
    h = rnd(y)
    mid = rnd(y - h)
    fine = h + mid
    th, tm, tl = split3(square(fine))
    far_h = jnp.where(is_pos, -2.0 * h, 0.0)
    far_m = jnp.where(is_pos, -2.0 * mid, 0.0)
    one = jnp.ones((1, WIDE), f32)
    ct = pick({0: one, 1: one, 2: one, 3: th, 4: tm, 5: tl}, (8, WIDE))
    target = jnp.concatenate([far_h, far_h, far_m, far_m, ct], axis=0).astype(bf16)
    total = jnp.zeros((WIDE, 16), f32)
    for k in range(4):
        raw = first if k == 0 else load(ids[k])
        ys = raw - origin
        sh = rnd(ys)
        sm = rnd(ys - sh)
        sf = sh + sm
        qh, qm, ql = split3(square(sf) + soften)
        cs = pick({0: qh, 1: qm, 2: ql, 3: one, 4: one, 5: one}, (8, WIDE))
        source = jnp.concatenate([sh, sm, sh, sm, cs], axis=0)
        r = lax.rsqrt(dot(target, source, (0, 0)))
        w = (r * r * r).astype(bf16)
        z = jnp.where(is_pos, sf * raw[3:4], raw)
        zh, zm, zl = split3(z)
        left = jnp.concatenate([zh, zm, zl, jnp.zeros((4, WIDE), f32)], axis=0)
        total = total + dot(w, left, (1, 1))
    total = total.T
    s = total[0:4] + total[4:8] + total[8:12]
    return s - fine * s[3:4]


def far_item(cells, origin, y):
    o = [jnp.broadcast_to(origin[i : i + 1, 0:1], (1, 128)) for i in range(3)]
    mass = cells[0:1]
    px, py, pz = [cells[1 + c : 2 + c] + cells[11 + c : 12 + c] - o[c] for c in range(3)]
    trace = cells[4:5] + cells[5:6] + cells[6:7]
    qxx, qyy, qzz = [3.0 * cells[i : i + 1] - trace for i in (4, 5, 6)]
    qxy, qxz, qyz = [3.0 * cells[i : i + 1] for i in (7, 8, 9)]
    gx = qxx * px + qxy * py + qxz * pz
    gy = qxy * px + qyy * py + qyz * pz
    gz = qxz * px + qyz * py + qzz * pz
    one = jnp.ones((1, 128), f32)
    pp = px * px + py * py + pz * pz + soften
    cs = pick({0: pp, 1: -2.0 * px, 2: -2.0 * py, 3: -2.0 * pz, 4: one, 5: one, 6: one}, (16, 128))
    pg = px * gx + py * gy + pz * gz
    cq = pick(
        {0: pg, 1: -2.0 * gx, 2: -2.0 * gy, 3: -2.0 * gz, 4: qxx, 5: qyy, 6: qzz, 7: 2.0 * qxy, 8: 2.0 * qxz, 9: 2.0 * qyz},
        (16, 128),
    )
    c = jnp.concatenate([cs, cq], axis=1)
    a, b, d = y[0:1], y[1:2], y[2:3]
    ones = jnp.ones((1, WIDE), f32)
    phi = pick(
        {0: ones, 1: a, 2: b, 3: d, 4: a * a, 5: b * b, 6: d * d, 7: a * b, 8: a * d, 9: b * d}, (16, WIDE)
    )
    ch, cm, cl = split3(c)
    fh, fm, fl = split3(phi)
    sq = dot(
        jnp.concatenate([ch, ch, cm, cm, ch, cl], axis=0),
        jnp.concatenate([fh, fm, fh, fm, fl, fh], axis=0),
        (0, 0),
    )
    s, q = sq[0:128], sq[128:256]
    r = lax.rsqrt(s)
    r2 = r * r
    r3 = r * r2
    r5 = r3 * r2
    l1 = pick({0: mass * px, 1: mass * py, 2: mass * pz, 3: -mass}, (16, 128))
    l2 = pick({0: 2.5 * px, 1: 2.5 * py, 2: 2.5 * pz, 3: -2.5 * one}, (16, 128))
    l3 = pick({0: -gx, 1: -gy, 2: -gz, 4: qxx, 5: qyy, 6: qzz, 7: qxy, 8: qxz, 9: qyz}, (16, 128))
    out = jnp.zeros((32, WIDE), f32)
    for l, v in ((l1, r3), (l2, q * (r5 * r2)), (l3, r5)):
        lh = rnd(l)
        pieces = jnp.concatenate([lh, rnd(l - lh)], axis=0)
        vh = v.astype(bf16)
        vm = (v - vh.astype(f32)).astype(bf16)
        out = out + dot(
            jnp.concatenate([pieces, pieces], axis=1), jnp.concatenate([vh, vm], axis=0), (1, 0)
        )
    t = out[0:16] + out[16:32]
    axx, ayy, azz, axy, axz, ayz = [t[i : i + 1] for i in range(4, 10)]
    turned = pick(
        {0: axx * a + axy * b + axz * d, 1: axy * a + ayy * b + ayz * d, 2: axz * a + ayz * b + azz * d}, (4, WIDE)
    )
    return t[0:4] + t[3:4] * y + turned


def top_values(t, ids):
    mass = t[0:1]
    own = t[10:11].astype(i32)
    d = [t[1 + c : 2 + c] - at for c, at in enumerate(centre(own))]
    md = [mass * d[c] for c in range(3)]
    rows = {0: mass, 1: md[0], 2: md[1], 3: md[2]}
    for k, (a, b) in enumerate(PAIRS):
        rows[4 + k] = t[4 + k : 5 + k] + md[a] * d[b]
    pieces = jnp.concatenate(split3(pick(rows, (16, BUCKETS))), axis=0)
    return pieces, jnp.where(ids == own, 1.0, 0.0)


def top_record(t, base):
    mass = t[0:1]
    w = jnp.maximum(mass, mass_floor)
    at = centre(lax.broadcasted_iota(i32, (1, 32), 1) + base)
    u = [t[1 + c : 2 + c] / w for c in range(3)]
    rows = {0: mass}
    for c in range(3):
        rows[1 + c] = at[c] + u[c]
    for k, (a, b) in enumerate(PAIRS):
        rows[4 + k] = t[4 + k : 5 + k] - t[1 + a : 2 + a] * u[b]
    return pick(rows, (16, 32))


def by_core(s):
    return (s & 1) * (SUB // 2) + (s >> 1)


def forced(force, slot):
    k = jnp.maximum(slot, 0)
    rows = [force[k >> 8, (k >> 6) & 3, c, pl.ds(k & 63, 1), :] for c in range(3)]
    return jnp.where(slot >= 0, jnp.concatenate(rows, axis=0), 0.0)


def kernel(
    work, pos_in, vel_in, acc_in, act_in, mass_in, top_row, cell_list, top_list, near_list, requests, work_row,
    vel_out, pos_out,
    pos, vel, acc, act, mass, half, dense, x, ahead,
    table_1, top_1, part_1, force_1, table_2, top_2, part_2, force_2,
    sums, pieces, top_pieces, cells, pairs,
    lists, wanted, codes, row, lane, tops, slots, near_s, work_s, slot_s,
    load_sem, send_sem, recv_sem, local_sem,
):
    g, s = lax.axis_index("dom"), lax.axis_index("sub")
    core, chip = lax.rem(s, 2), s // 2
    sibling = (g, s + 1 - 2 * core)
    up, down, over = [(g, lax.rem(s + k, SUB)) for k in (2, 6, 4)]
    along = [up, down, over]
    across = [(lax.rem(g + k, DOM), s) for k in range(1, DOM)]
    within = [(g, lax.rem(s + k, SUB)) for k in range(1, SUB)]
    used = [0]

    inputs = [
        pltpu.make_async_copy(a, b, load_sem.at[k])
        for k, (a, b) in enumerate(((pos_in, pos), (vel_in, vel), (acc_in, acc), (act_in, act), (mass_in, mass)))
    ]
    for c in inputs:
        c.start()

    barrier = pltpu.get_barrier_semaphore()
    for peer in across + within:
        pl.semaphore_signal(barrier, inc=1, device_id=peer, device_id_type=MESH)
    def send(ref, peers, source=None):
        copies = []
        for peer in peers:
            k = used[0]
            used[0] += 1
            copies.append(
                pltpu.make_async_remote_copy(
                    src_ref=ref if source is None else source, dst_ref=ref, send_sem=send_sem.at[k],
                    recv_sem=recv_sem.at[k], device_id=peer, device_id_type=MESH,
                )
            )
            copies[-1].start()
        return copies

    def done(copies):
        for c in copies:
            c.wait()

    below, above, facing = [lax.rem(chip + k, 4) for k in (3, 1, 2)]
    low, high = pl.ds(0, BUCKETS // 2), pl.ds(BUCKETS // 2, BUCKETS // 2)

    def ring_1(buf):
        return send(buf.at[core, chip], [up, down, sibling])

    def ring_2(buf, first):
        first[0].wait_recv()
        found = send(buf.at[core, below, low], [up])
        more = send(buf.at[core, below], [sibling])
        first[1].wait_recv()
        found += send(buf.at[core, above, high], [down])
        more += send(buf.at[core, above], [sibling])
        return found, more

    def ring_3(buf, first, second):
        found, more = second
        for c in found:
            c.wait_recv()
        final = send(buf.at[core, facing], [sibling])
        for c in first + found:
            c.wait_send()
        first[2].wait_recv()
        done(more)
        return final

    for c in inputs:
        c.wait()

    def first(b, carry):
        sl = pl.ds(pl.multiple_of(b * WIDE, WIDE), WIDE)
        a = act[:, sl].astype(f32)
        h = vel[:, sl] + kick * a * acc[:, sl]
        p = pos[:, sl] + time_step * h
        half[:, sl] = h
        m = mass[:, sl]
        x[core, chip, b] = jnp.concatenate([p, m], axis=0)
        ahead[core, chip, b] = jnp.concatenate([p + time_step * h, a], axis=0)
        for c in range(3):
            dense[c, pl.ds(b, 1), :] = p[c : c + 1]
        dense[3, pl.ds(b, 1), :] = m
        return carry

    lax.fori_loop(0, BUCKETS, first, 0, unroll=4)
    pl.semaphore_wait(barrier, DOM + SUB - 2)
    x_1 = ring_1(x)
    turned = [cell_list[...], top_list[...], near_list[...], jnp.zeros((28, BUCKETS), i32)]
    lists[core, chip, 0:BUCKETS, :] = jnp.concatenate(turned, axis=0).T
    asked = requests[...]
    asked = (by_core(asked >> 7) * DOM + row_iota((DOM, 32))) * 128 + (asked & 127)
    rest = [jnp.concatenate([asked[4 * r + k : 4 * r + k + 1] for k in range(4)], axis=1) for r in range(4)]
    rest.append(jnp.concatenate([work_row[...], jnp.full((1, 128 - ITEMS), -1, i32)], axis=1))
    lists[core, chip, BUCKETS : BUCKETS + 8, :] = jnp.concatenate(rest + [jnp.zeros((3, 128), i32)], axis=0)
    list_copies = send(lists.at[core, chip], along)

    def near_part(load, begin, end):
        def item(w, carry):
            pairs[w] = near_item(load, [near_s[w, NEAR_AT + k] for k in range(4)])
            return carry

        lax.fori_loop(begin, end, item, 0, unroll=4)

    def top_sums(table, part):
        base = (s * DOM + g) * 32
        ids = lax.broadcasted_iota(i32, (32, BUCKETS), 0) + base
        sums[...] = jnp.zeros_like(sums)

        def step(i, carry):
            at, k = i >> 2, (i & 3) * 4
            got = [top_values(table[at >> 2, at & 3, k + u], ids) for u in range(4)]
            v = jnp.concatenate([a for a, _ in got], axis=1)
            o = jnp.concatenate([b for _, b in got], axis=1)
            sums[...] += dot(v, o, (1, 1))
            return carry

        lax.fori_loop(0, SUB * DOM // 4, step, 0, unroll=4)
        mine = top_record(sums[0:16] + sums[16:32] + sums[32:48], base)
        four = jnp.concatenate([mine] * 4, axis=1)
        quarter = lax.broadcasted_iota(i32, (16, 128), 1) // 32
        part[g] = jnp.where(quarter == lax.rem(g, 4), four, 0.0)

    def four_parts(top, part):
        for k in range(4):
            top[s, k] = part[4 * k] + part[4 * k + 1] + part[4 * k + 2] + part[4 * k + 3]

    def essential_cells(table):
        spread(lambda k: table[k >> 6, (k >> 4) & 3, k & 15], pieces, SUB * DOM)

        def gather(i, carry):
            ess = lookup(pieces, SUB * DOM, row[pl.ds(i, 1), :], lane[pl.ds(i, 1), :])
            blank = jnp.zeros((16, 64), f32)
            for u in range(4):
                cells[i * 4 + u] = jnp.concatenate([ess[:, u * 64 : u * 64 + 64], blank], axis=1)
            return carry

        lax.fori_loop(0, ITEMS // 4, gather, 0, unroll=2)

    def top_cells(top):
        spread(lambda k: top[k >> 2, k & 3], top_pieces, 32)

        def gather(i, carry):
            t = tops[pl.ds(i, 1), :]
            far = lookup(top_pieces, 32, t >> 7, t & 127)
            blank = [jnp.zeros((16, n), f32) for n in (64, 32)]
            for u in range(8):
                cells[i * 8 + u] += jnp.concatenate([blank[0], far[:, u * 32 : u * 32 + 32], blank[1]], axis=1)
            return carry

        lax.fori_loop(0, ITEMS // 8, gather, 0, unroll=5)

    def finish(load, force, known, between=None):
        first_sem = used[0]
        used[0] += 16

        def copy(ref, k, peer):
            return pltpu.make_async_remote_copy(
                src_ref=ref, dst_ref=ref, send_sem=send_sem.at[k], recv_sem=recv_sem.at[k],
                device_id=peer, device_id_type=MESH,
            )

        def rows(p):
            return pl.ds(pl.multiple_of(p * 8, 8), 8)

        def by_links(p):
            ref = force.at[core, chip, :, rows(p), :]
            return [copy(ref, first_sem + p * 3 + k, peer) for k, peer in enumerate(along)]

        def to_sibling(p):
            return copy(force.at[core, :, :, rows(p), :], first_sem + 12 + p, sibling)

        def forward(p):
            done(by_links(p))
            to_sibling(p).start()

        def compute(p, with_near):
            def item(i, carry):
                w = p * 8 + i
                _, origin, y = from_first(load(near_s[w, NEAR_AT]))
                if with_near:
                    a = near_item(load, [near_s[w, NEAR_AT + k] for k in range(4)])
                else:
                    a = pairs[w]
                a = a + far_item(cells[w], origin, y)
                for c in range(3):
                    force[core, chip, c, pl.ds(w, 1), :] = a[c : c + 1]
                return carry

            lax.fori_loop(0, 8, item, 0, unroll=4)

        def piece(p, carry, with_near):
            compute(p, with_near)
            for c in by_links(p):
                c.start()

            @pl.when(p > 0)
            def _():
                forward(p - 1)

            return carry

        if known:
            lax.fori_loop(0, known // 8, functools.partial(piece, with_near=False), 0)
        if known < 24:
            lax.fori_loop(known // 8, 3, functools.partial(piece, with_near=True), 0)
        middle = between() if between else None
        lax.fori_loop(3, 4, functools.partial(piece, with_near=True), 0)
        compute(4, True)
        final = send(force.at[core, chip, :, pl.ds(32, 8), :], within)
        forward(3)
        done(final)
        for p in range(4):
            to_sibling(p).wait()
        return middle

    moments(dense, top_row[...].astype(f32), table_1.at[core, chip, g])
    flight = send(table_1.at[core, chip, g], along)
    done(flight)
    flight = send(table_1.at[core, :, g], across)
    done(list_copies)
    list_copies = send(lists.at[core], [sibling])
    x_2 = ring_2(x, x_1)
    done(list_copies)

    def take(w, carry):
        n = work[w]
        wanted[pl.ds(w, 1), :] = lists[(n >> 7) & 1, n >> 8, pl.ds(n & 127, 1), :]
        return carry

    lax.fori_loop(0, ITEMS, take, 0, unroll=4)
    to_scalars = [pltpu.make_async_copy(wanted, near_s, local_sem.at[0])]
    for k in range(SUB):
        to_scalars.append(
            pltpu.make_async_copy(lists.at[k // 4, k % 4, pl.ds(128, 8)], work_s.at[k], local_sem.at[1 + k])
        )
    for c in to_scalars:
        c.start()
    for k in range(SUB):
        codes[4 * k : 4 * k + 4, :] = lists[k % 2, k // 2, 128:132, :]

    def place(i, carry):
        ids = jnp.concatenate([wanted[pl.ds(4 * i + u, 1), :][:, 0:64] for u in range(4)], axis=1)
        hot = jnp.where(row_iota((128, 256)) == (ids & 127), 1.0, 0.0)
        at = row_iota((32, 256)) == (ids >> 7)
        for got, where in ((codes[...] >> 7, row), (codes[...] & 127, lane)):
            found = dot(got.astype(f32), hot, (1, 0))
            where[pl.ds(i, 1), :] = jnp.sum(jnp.where(at, found, 0.0), axis=0, keepdims=True).astype(i32)
        return carry

    lax.fori_loop(0, ITEMS // 4, place, 0, unroll=5)
    for i in range(ITEMS // 8):
        tops[i : i + 1, :] = jnp.concatenate([wanted[8 * i + u : 8 * i + u + 1, 64:96] for u in range(8)], axis=1)
    for c in to_scalars:
        c.wait()
    number = row_iota((SUB, 128)) * 128 + lax.broadcasted_iota(i32, (SUB, 128), 1)

    def find(w, found):
        for k in range(SUB):
            found = jnp.where(number == work_s[k, 4, w], k * 64 + w, found)
        return found

    slots[...] = lax.fori_loop(0, ITEMS, find, jnp.full((SUB, 128), -1, i32), unroll=4)
    slot_copy = pltpu.make_async_copy(slots, slot_s, local_sem.at[9])
    slot_copy.start()

    done(flight)
    flight = send(table_1.at[core], [sibling])
    x_3 = ring_3(x, x_1, x_2)
    done(flight)
    top_sums(table_1, part_1)
    flight = send(part_1.at[g], across)
    essential_cells(table_1)
    done(flight)
    four_parts(top_1, part_1)
    flight = send(top_1.at[s], within)
    done(x_3)
    ahead_1 = ring_1(ahead)
    slot_copy.wait()

    def load_1(n):
        return x[(n >> 7) & 1, n >> 8, n & 127]

    near_part(load_1, 0, 8)
    done(flight)
    top_cells(top_1)
    ahead_2 = finish(load_1, force_1, 8, lambda: ring_2(ahead, ahead_1))

    def second(b, carry):
        sl = pl.ds(pl.multiple_of(b * WIDE, WIDE), WIDE)
        push = kick * act[:, sl].astype(f32) * forced(force_1, slot_s[s, b])
        h = half[:, sl] + push + push
        p = x[core, chip, b][0:3] + time_step * h
        half[:, sl] = h
        pos_out[:, sl] = p
        for c in range(3):
            dense[c, pl.ds(b, 1), :] = p[c : c + 1]
        return carry

    lax.fori_loop(0, BUCKETS, second, 0, unroll=4)
    moments(dense, top_row[...].astype(f32), table_2.at[core, chip, g])
    flight = send(table_2.at[core, chip, g], along)
    ahead_3 = ring_3(ahead, ahead_1, ahead_2)
    done(flight)
    flight = send(table_2.at[core, :, g], across)
    done(ahead_3)

    def load_2(n):
        at = ((n >> 7) & 1, n >> 8, n & 127)
        p = ahead[at]
        moved = p[0:3] + (2.0 * kick * time_step) * p[3:4] * forced(force_1, slot_s[n >> 7, n & 127])
        return jnp.concatenate([moved, x[at][3:4]], axis=0)

    near_part(load_2, 0, 12)
    done(flight)
    flight = send(table_2.at[core], [sibling])
    near_part(load_2, 12, 20)
    done(flight)
    top_sums(table_2, part_2)
    flight = send(part_2.at[g], across)
    essential_cells(table_2)
    done(flight)
    four_parts(top_2, part_2)
    flight = send(top_2.at[s], within)
    near_part(load_2, 20, 24)
    done(flight)
    top_cells(top_2)
    finish(load_2, force_2, 24)

    def last(b, carry):
        sl = pl.ds(pl.multiple_of(b * WIDE, WIDE), WIDE)
        vel_out[:, sl] = half[:, sl] + kick * act[:, sl].astype(f32) * forced(force_2, slot_s[s, b])
        return carry

    lax.fori_loop(0, BUCKETS, last, 0, unroll=4)


def body(positions, velocities, masses, accel_prev, active, bucket_top, near_list, cell_list, top_list, essential, work):
    n = positions.shape[1]
    vm, dma = pltpu.VMEM, pltpu.SemaphoreType.DMA
    flat = vm((3, n), f32)
    group = vm((2, SUB // 2, BUCKETS, 4, WIDE), f32)
    twice = [
        vm((2, SUB // 2, DOM, 16, 128), f32), vm((SUB, 4, 16, 128), f32), vm((DOM, 16, 128), f32),
        vm((2, SUB // 2, 3, ITEMS, WIDE), f32),
    ]
    scratch = [flat, flat, flat, vm((1, n), i32), vm((1, n), f32), flat, vm((4, BUCKETS, WIDE), f32), group, group]
    scratch += twice + twice
    scratch += [
        vm((48, 32), f32), vm((SUB * DOM * 16, 256), bf16), vm((32 * 16, 256), bf16),
        vm((ITEMS, 16, 128), f32), vm((ITEMS, 4, WIDE), f32),
        vm((2, SUB // 2, BUCKETS + 8, 128), i32), vm((ITEMS, 128), i32), vm((32, 128), i32),
        vm((16, 256), i32), vm((16, 256), i32), vm((8, 256), i32), vm((SUB, 128), i32),
        pltpu.SMEM((ITEMS, 128), i32), pltpu.SMEM((SUB, 8, 128), i32), pltpu.SMEM((SUB, 128), i32),
        dma((5,)), dma((COPIES,)), dma((COPIES,)), dma((10,)),
    ]
    place = lambda where: pl.BlockSpec(memory_space=where)
    shape = jax.ShapeDtypeStruct((3, n), f32)
    return pl.pallas_call(
        kernel,
        out_shape=(shape, shape),
        in_specs=[place(pltpu.SMEM)] + [place(pltpu.HBM)] * 5 + [place(pltpu.VMEM)] * 6,
        out_specs=(place(pltpu.VMEM), place(pltpu.VMEM)),
        scratch_shapes=scratch,
        compiler_params=pltpu.CompilerParams(collective_id=1, has_side_effects=True, vmem_limit_bytes=62 * MIB),
    )(
        work, positions, velocities, accel_prev, active.reshape(1, n), masses.reshape(1, n),
        bucket_top.reshape(1, BUCKETS), cell_list.T, top_list.T, near_list.T, essential.reshape(DOM, -1),
        work.reshape(1, ITEMS),
    )


def solution(mesh):
    both = ("dom", "sub")
    in_specs = (
        P(None, both), P(None, both), P(both), P(None, both), P(both), P(both),
        P(both, None), P(both, None), P(both, None), P("dom", "sub", None, None), P(both),
    )
    return jax.shard_map(
        body, mesh=mesh, in_specs=in_specs, out_specs=(P(None, both), P(None, both)), check_vma=False
    )
```

```python
import functools

import jax
import jax.numpy as jnp
from jax import lax
from jax.experimental import pallas as pl
from jax.experimental.pallas import tpu as pltpu
from jax.sharding import PartitionSpec as P

f32, bf16, i32 = jnp.float32, jnp.bfloat16, jnp.int32
MESH = pl.DeviceIdType.MESH
SUB, DOM = 8, 16
BUCKETS, WIDE, ITEMS = 128, 256, 40
GROUP = SUB * BUCKETS
TOP_SIDE = 16
MIB = 2**20

time_step = 0.01
soften = 0.0025
mass_floor = 0.5
kick = 0.5 * time_step
PAIRS = ((0, 0), (1, 1), (2, 2), (0, 1), (0, 2), (1, 2))
NEAR_AT = 96
COPIES = 160


def rnd(a):
    return a.astype(bf16).astype(f32)


def split3(a):
    h = rnd(a)
    r = a - h
    m = rnd(r)
    return h, m, rnd(r - m)


def dot(a, b, dims):
    return lax.dot_general(
        a.astype(bf16), b.astype(bf16), ((dims[:1], dims[1:]), ((), ())), preferred_element_type=f32
    )


def row_iota(shape):
    return lax.broadcasted_iota(i32, shape, 0)


def pick(rows, shape):
    at = row_iota(shape)
    out = jnp.zeros(shape, f32)
    for i, v in rows.items():
        out = jnp.where(at == i, v, out)
    return out


def square(y):
    q = y * y
    return q[0:1] + q[1:2] + q[2:3]


def moments(dense, top_row, rec_ref):
    first = [dense[c][:, 0:1] for c in range(3)]
    y = [dense[c] - first[c] for c in range(3)]
    m = dense[3]
    ones = jnp.ones((16, WIDE), f32)
    lead = jnp.where(lax.broadcasted_iota(i32, (16, WIDE), 1) == 0, 1.0, 0.0)

    def total(a, by=ones):
        h, m, l = split3(a)
        return (dot(by, h, (1, 1)) + (dot(by, m, (1, 1)) + dot(by, l, (1, 1))))[0:1]

    my = [m * y[c] for c in range(3)]
    mass = total(m)
    start = [total(dense[c], lead) for c in range(3)]
    s = [total(my[c]) for c in range(3)]
    d = [s[c] / mass for c in range(3)]
    second = [total(my[a] * y[b]) - s[a] * d[b] for a, b in PAIRS]
    rows = {0: mass, 10: top_row}
    for c in range(3):
        rows[1 + c] = start[c] + d[c]
    for k in range(6):
        rows[4 + k] = second[k]
    rec_ref[...] = pick(rows, (16, BUCKETS))


def centre(ids):
    return [
        (part.astype(f32) + 0.5) / TOP_SIDE
        for part in (ids >> 8, (ids >> 4) & 15, ids & 15)
    ]


def spread(table, pieces, rows):
    at = row_iota((16, 128))
    extra = (at >= 11) & (at < 14)

    def step(k, carry):
        t = table(k)
        h, m, l = split3(t)
        low = pltpu.roll(l, 10, 0)
        both = jnp.concatenate([jnp.where(extra, low, h), jnp.where(extra, 0.0, m)], axis=1)
        pieces[pl.ds(pl.multiple_of(k * 16, 16), 16), :] = both.astype(bf16)
        return carry

    lax.fori_loop(0, rows, step, 0, unroll=4)


def lookup(pieces, rows, row, lane):
    n = row.shape[1]
    hot = jnp.where(row_iota((128, n)) == lane, 1.0, 0.0).astype(bf16)
    hot = jnp.concatenate([hot, hot], axis=0)
    row16 = jnp.broadcast_to(row, (16, n))

    def step(i, got):
        block = pieces[pl.ds(pl.multiple_of(i * 128, 128), 128), :]
        found = dot(block, hot, (1, 0))
        for u in range(8):
            got = jnp.where(row16 == i * 8 + u, found[u * 16 : u * 16 + 16], got)
        return got

    return lax.fori_loop(0, rows // 8, step, jnp.zeros((16, n), f32), unroll=rows // 8)


def from_first(first):
    is_pos = row_iota((4, WIDE)) < 3
    origin = jnp.where(is_pos, jnp.broadcast_to(first[:, 0:1], (4, WIDE)), 0.0)
    return is_pos, origin, first - origin


def near_item(load, ids):
    first = load(ids[0])
    is_pos, origin, y = from_first(first)
    h = rnd(y)
    mid = rnd(y - h)
    fine = h + mid
    th, tm, tl = split3(square(fine))
    far_h = jnp.where(is_pos, -2.0 * h, 0.0)
    far_m = jnp.where(is_pos, -2.0 * mid, 0.0)
    one = jnp.ones((1, WIDE), f32)
    ct = pick({0: one, 1: one, 2: one, 3: th, 4: tm, 5: tl}, (8, WIDE))
    target = jnp.concatenate([far_h, far_h, far_m, far_m, ct], axis=0).astype(bf16)
    total = jnp.zeros((WIDE, 16), f32)
    for k in range(4):
        raw = first if k == 0 else load(ids[k])
        ys = raw - origin
        sh = rnd(ys)
        sm = rnd(ys - sh)
        sf = sh + sm
        qh, qm, ql = split3(square(sf) + soften)
        cs = pick({0: qh, 1: qm, 2: ql, 3: one, 4: one, 5: one}, (8, WIDE))
        source = jnp.concatenate([sh, sm, sh, sm, cs], axis=0)
        r = lax.rsqrt(dot(target, source, (0, 0)))
        w = (r * r * r).astype(bf16)
        z = jnp.where(is_pos, sf * raw[3:4], raw)
        zh, zm, zl = split3(z)
        left = jnp.concatenate([zh, zm, zl, jnp.zeros((4, WIDE), f32)], axis=0)
        total = total + dot(w, left, (1, 1))
    total = total.T
    s = total[0:4] + total[4:8] + total[8:12]
    return s - fine * s[3:4]


def far_item(cells, origin, y):
    o = [jnp.broadcast_to(origin[i : i + 1, 0:1], (1, 128)) for i in range(3)]
    mass = cells[0:1]
    px, py, pz = [cells[1 + c : 2 + c] + cells[11 + c : 12 + c] - o[c] for c in range(3)]
    trace = cells[4:5] + cells[5:6] + cells[6:7]
    qxx, qyy, qzz = [3.0 * cells[i : i + 1] - trace for i in (4, 5, 6)]
    qxy, qxz, qyz = [3.0 * cells[i : i + 1] for i in (7, 8, 9)]
    gx = qxx * px + qxy * py + qxz * pz
    gy = qxy * px + qyy * py + qyz * pz
    gz = qxz * px + qyz * py + qzz * pz
    one = jnp.ones((1, 128), f32)
    pp = px * px + py * py + pz * pz + soften
    cs = pick({0: pp, 1: -2.0 * px, 2: -2.0 * py, 3: -2.0 * pz, 4: one, 5: one, 6: one}, (16, 128))
    pg = px * gx + py * gy + pz * gz
    cq = pick(
        {0: pg, 1: -2.0 * gx, 2: -2.0 * gy, 3: -2.0 * gz, 4: qxx, 5: qyy, 6: qzz, 7: 2.0 * qxy, 8: 2.0 * qxz, 9: 2.0 * qyz},
        (16, 128),
    )
    c = jnp.concatenate([cs, cq], axis=1)
    a, b, d = y[0:1], y[1:2], y[2:3]
    ones = jnp.ones((1, WIDE), f32)
    phi = pick(
        {0: ones, 1: a, 2: b, 3: d, 4: a * a, 5: b * b, 6: d * d, 7: a * b, 8: a * d, 9: b * d}, (16, WIDE)
    )
    ch, cm, cl = split3(c)
    fh, fm, fl = split3(phi)
    sq = dot(
        jnp.concatenate([fh, fm, fh, fm, fl, fh], axis=0),
        jnp.concatenate([ch, ch, cm, cm, ch, cl], axis=0),
        (0, 0),
    )
    s, q = sq[:, 0:128], sq[:, 128:256]
    r = lax.rsqrt(s)
    r2 = r * r
    r3 = r * r2
    r5 = r3 * r2
    l1 = pick({0: mass * px, 1: mass * py, 2: mass * pz, 3: -mass}, (16, 128))
    l2 = pick({0: 2.5 * px, 1: 2.5 * py, 2: 2.5 * pz, 3: -2.5 * one}, (16, 128))
    l3 = pick({0: -gx, 1: -gy, 2: -gz, 4: qxx, 5: qyy, 6: qzz, 7: qxy, 8: qxz, 9: qyz}, (16, 128))
    out = jnp.zeros((WIDE, 32), f32)
    for l, v in ((l1, r3), (l2, q * (r5 * r2)), (l3, r5)):
        lh = rnd(l)
        pieces = jnp.concatenate([lh, rnd(l - lh)], axis=0)
        vh = v.astype(bf16)
        vm = (v - vh.astype(f32)).astype(bf16)
        out = out + dot(
            jnp.concatenate([vh, vm], axis=1), jnp.concatenate([pieces, pieces], axis=1), (1, 1)
        )
    out = out.T
    t = out[0:16] + out[16:32]
    axx, ayy, azz, axy, axz, ayz = [t[i : i + 1] for i in range(4, 10)]
    turned = pick(
        {0: axx * a + axy * b + axz * d, 1: axy * a + ayy * b + ayz * d, 2: axz * a + ayz * b + azz * d}, (4, WIDE)
    )
    return t[0:4] + t[3:4] * y + turned


def top_values(t, ids):
    mass = t[0:1]
    own = t[10:11].astype(i32)
    d = [t[1 + c : 2 + c] - at for c, at in enumerate(centre(own))]
    md = [mass * d[c] for c in range(3)]
    rows = {0: mass, 1: md[0], 2: md[1], 3: md[2]}
    for k, (a, b) in enumerate(PAIRS):
        rows[4 + k] = t[4 + k : 5 + k] + md[a] * d[b]
    pieces = jnp.concatenate(split3(pick(rows, (16, BUCKETS))), axis=0)
    return pieces, jnp.where(ids == own, 1.0, 0.0)


def top_record(t, base):
    mass = t[0:1]
    w = jnp.maximum(mass, mass_floor)
    at = centre(lax.broadcasted_iota(i32, (1, 32), 1) + base)
    u = [t[1 + c : 2 + c] / w for c in range(3)]
    rows = {0: mass}
    for c in range(3):
        rows[1 + c] = at[c] + u[c]
    for k, (a, b) in enumerate(PAIRS):
        rows[4 + k] = t[4 + k : 5 + k] - t[1 + a : 2 + a] * u[b]
    return pick(rows, (16, 32))


def by_core(s):
    return (s & 1) * (SUB // 2) + (s >> 1)


def forced(force, slot):
    k = jnp.maximum(slot, 0)
    rows = [force[k >> 8, (k >> 6) & 3, c, pl.ds(k & 63, 1), :] for c in range(3)]
    return jnp.where(slot >= 0, jnp.concatenate(rows, axis=0), 0.0)


def kernel(
    work, pos_in, vel_in, acc_in, act_in, mass_in, top_row, cell_list, top_list, near_list, requests, work_row,
    vel_out, pos_out,
    pos, vel, acc, act, mass, half, dense, x, ahead,
    table_1, top_1, part_1, force_1, table_2, top_2, part_2, force_2,
    sums, pieces, top_pieces, cells, pairs,
    lists, wanted, codes, row, lane, tops, slots, near_s, work_s, slot_s,
    load_sem, send_sem, recv_sem, local_sem,
):
    g, s = lax.axis_index("dom"), lax.axis_index("sub")
    core, chip = lax.rem(s, 2), s // 2
    sibling = (g, s + 1 - 2 * core)
    up, down, over = [(g, lax.rem(s + k, SUB)) for k in (2, 6, 4)]
    along = [up, down, over]
    across = [(lax.rem(g + k, DOM), s) for k in range(1, DOM)]
    within = [(g, lax.rem(s + k, SUB)) for k in range(1, SUB)]
    used = [0]

    inputs = [
        pltpu.make_async_copy(a, b, load_sem.at[k])
        for k, (a, b) in enumerate(((pos_in, pos), (vel_in, vel), (acc_in, acc), (act_in, act), (mass_in, mass)))
    ]
    for c in inputs:
        c.start()

    barrier = pltpu.get_barrier_semaphore()
    for peer in across + within:
        pl.semaphore_signal(barrier, inc=1, device_id=peer, device_id_type=MESH)
    def send(ref, peers, source=None):
        copies = []
        for peer in peers:
            k = used[0]
            used[0] += 1
            copies.append(
                pltpu.make_async_remote_copy(
                    src_ref=ref if source is None else source, dst_ref=ref, send_sem=send_sem.at[k],
                    recv_sem=recv_sem.at[k], device_id=peer, device_id_type=MESH,
                )
            )
            copies[-1].start()
        return copies

    def done(copies):
        for c in copies:
            c.wait()

    below, above, facing = [lax.rem(chip + k, 4) for k in (3, 1, 2)]
    low, high = pl.ds(0, BUCKETS // 2), pl.ds(BUCKETS // 2, BUCKETS // 2)

    def ring_1(buf):
        return send(buf.at[core, chip], [up, down, sibling])

    def ring_2(buf, first):
        first[0].wait_recv()
        found = send(buf.at[core, below, low], [up])
        more = send(buf.at[core, below], [sibling])
        first[1].wait_recv()
        found += send(buf.at[core, above, high], [down])
        more += send(buf.at[core, above], [sibling])
        return found, more

    def ring_3(buf, first, second):
        found, more = second
        for c in found:
            c.wait_recv()
        final = send(buf.at[core, facing], [sibling])
        for c in first + found:
            c.wait_send()
        first[2].wait_recv()
        done(more)
        return final

    for c in inputs:
        c.wait()

    def first(b, carry):
        sl = pl.ds(pl.multiple_of(b * WIDE, WIDE), WIDE)
        a = act[:, sl].astype(f32)
        h = vel[:, sl] + kick * a * acc[:, sl]
        p = pos[:, sl] + time_step * h
        half[:, sl] = h
        x[core, chip, b] = jnp.concatenate([p, mass[:, sl]], axis=0)
        return carry

    lax.fori_loop(0, BUCKETS, first, 0, unroll=8)
    pl.semaphore_wait(barrier, DOM + SUB - 2)
    x_1 = ring_1(x)

    def onward(b, carry):
        sl = pl.ds(pl.multiple_of(b * WIDE, WIDE), WIDE)
        p = x[core, chip, b]
        next_p = p[0:3] + time_step * half[:, sl]
        ahead[core, chip, b] = jnp.concatenate([next_p, act[:, sl].astype(f32)], axis=0)
        for c in range(4):
            dense[c, pl.ds(b, 1), :] = p[c : c + 1]
        return carry

    lax.fori_loop(0, BUCKETS, onward, 0, unroll=8)
    turned = [cell_list[...], top_list[...], near_list[...], jnp.zeros((28, BUCKETS), i32)]
    lists[core, chip, 0:BUCKETS, :] = jnp.concatenate(turned, axis=0).T
    asked = requests[...]
    asked = (by_core(asked >> 7) * DOM + row_iota((DOM, 32))) * 128 + (asked & 127)
    rest = [jnp.concatenate([asked[4 * r + k : 4 * r + k + 1] for k in range(4)], axis=1) for r in range(4)]
    rest.append(jnp.concatenate([work_row[...], jnp.full((1, 128 - ITEMS), -1, i32)], axis=1))
    lists[core, chip, BUCKETS : BUCKETS + 8, :] = jnp.concatenate(rest + [jnp.zeros((3, 128), i32)], axis=0)
    list_copies = send(lists.at[core, chip], along)

    def near_part(load, begin, end):
        def item(w, carry):
            pairs[w] = near_item(load, [near_s[w, NEAR_AT + k] for k in range(4)])
            return carry

        lax.fori_loop(begin, end, item, 0, unroll=4)

    def top_sums(table, part):
        base = (s * DOM + g) * 32
        ids = lax.broadcasted_iota(i32, (32, BUCKETS), 0) + base
        sums[...] = jnp.zeros_like(sums)

        def step(i, carry):
            at, k = i >> 2, (i & 3) * 4
            got = [top_values(table[at >> 2, at & 3, k + u], ids) for u in range(4)]
            v = jnp.concatenate([a for a, _ in got], axis=1)
            o = jnp.concatenate([b for _, b in got], axis=1)
            sums[...] += dot(v, o, (1, 1))
            return carry

        lax.fori_loop(0, SUB * DOM // 4, step, 0, unroll=4)
        mine = top_record(sums[0:16] + sums[16:32] + sums[32:48], base)
        four = jnp.concatenate([mine] * 4, axis=1)
        quarter = lax.broadcasted_iota(i32, (16, 128), 1) // 32
        part[g] = jnp.where(quarter == lax.rem(g, 4), four, 0.0)

    def four_parts(top, part):
        for k in range(4):
            top[s, k] = part[4 * k] + part[4 * k + 1] + part[4 * k + 2] + part[4 * k + 3]

    def essential_cells(table):
        spread(lambda k: table[k >> 6, (k >> 4) & 3, k & 15], pieces, SUB * DOM)

        def gather(i, carry):
            ess = lookup(pieces, SUB * DOM, row[pl.ds(i, 1), :], lane[pl.ds(i, 1), :])
            blank = jnp.zeros((16, 64), f32)
            for u in range(4):
                cells[i * 4 + u] = jnp.concatenate([ess[:, u * 64 : u * 64 + 64], blank], axis=1)
            return carry

        lax.fori_loop(0, ITEMS // 4, gather, 0, unroll=2)

    def top_cells(top):
        spread(lambda k: top[k >> 2, k & 3], top_pieces, 32)

        def gather(i, carry):
            t = tops[pl.ds(i, 1), :]
            far = lookup(top_pieces, 32, t >> 7, t & 127)
            blank = [jnp.zeros((16, n), f32) for n in (64, 32)]
            for u in range(8):
                cells[i * 8 + u] += jnp.concatenate([blank[0], far[:, u * 32 : u * 32 + 32], blank[1]], axis=1)
            return carry

        lax.fori_loop(0, ITEMS // 8, gather, 0, unroll=5)

    def finish(load, force, known, between=None):
        first_sem = used[0]
        used[0] += 16

        def copy(ref, k, peer):
            return pltpu.make_async_remote_copy(
                src_ref=ref, dst_ref=ref, send_sem=send_sem.at[k], recv_sem=recv_sem.at[k],
                device_id=peer, device_id_type=MESH,
            )

        def rows(p):
            return pl.ds(pl.multiple_of(p * 8, 8), 8)

        def by_links(p):
            ref = force.at[core, chip, :, rows(p), :]
            return [copy(ref, first_sem + p * 3 + k, peer) for k, peer in enumerate(along)]

        def to_sibling(p):
            return copy(force.at[core, :, :, rows(p), :], first_sem + 12 + p, sibling)

        def forward(p):
            done(by_links(p))
            to_sibling(p).start()

        def compute(p, with_near):
            def item(i, carry):
                w = p * 8 + i
                _, origin, y = from_first(load(near_s[w, NEAR_AT]))
                if with_near:
                    a = near_item(load, [near_s[w, NEAR_AT + k] for k in range(4)])
                else:
                    a = pairs[w]
                a = a + far_item(cells[w], origin, y)
                for c in range(3):
                    force[core, chip, c, pl.ds(w, 1), :] = a[c : c + 1]
                return carry

            lax.fori_loop(0, 8, item, 0, unroll=4)

        def piece(p, carry, with_near):
            compute(p, with_near)
            for c in by_links(p):
                c.start()

            @pl.when(p > 0)
            def _():
                forward(p - 1)

            return carry

        if known:
            lax.fori_loop(0, known // 8, functools.partial(piece, with_near=False), 0)
        if known < 24:
            lax.fori_loop(known // 8, 3, functools.partial(piece, with_near=True), 0)
        middle = between() if between else None
        lax.fori_loop(3, 4, functools.partial(piece, with_near=True), 0)
        compute(4, True)
        final = send(force.at[core, chip, :, pl.ds(32, 8), :], within)
        forward(3)
        done(final)
        for p in range(4):
            to_sibling(p).wait()
        return middle

    moments(dense, top_row[...].astype(f32), table_1.at[core, chip, g])
    flight = send(table_1.at[core, chip, g], along)
    done(flight)
    flight = send(table_1.at[core, :, g], across)
    done(list_copies)
    list_copies = send(lists.at[core], [sibling])
    x_2 = ring_2(x, x_1)
    done(flight)
    flight = send(table_1.at[core], [sibling])
    done(list_copies)

    def take(w, carry):
        n = work[w]
        wanted[pl.ds(w, 1), :] = lists[(n >> 7) & 1, n >> 8, pl.ds(n & 127, 1), :]
        return carry

    lax.fori_loop(0, ITEMS, take, 0, unroll=4)
    to_scalars = [pltpu.make_async_copy(wanted, near_s, local_sem.at[0])]
    for k in range(SUB):
        to_scalars.append(
            pltpu.make_async_copy(lists.at[k // 4, k % 4, pl.ds(128, 8)], work_s.at[k], local_sem.at[1 + k])
        )
    for c in to_scalars:
        c.start()
    for k in range(SUB):
        codes[4 * k : 4 * k + 4, :] = lists[k % 2, k // 2, 128:132, :]

    def place(i, carry):
        ids = jnp.concatenate([wanted[pl.ds(4 * i + u, 1), :][:, 0:64] for u in range(4)], axis=1)
        hot = jnp.where(row_iota((128, 256)) == (ids & 127), 1.0, 0.0)
        at = row_iota((32, 256)) == (ids >> 7)
        for got, where in ((codes[...] >> 7, row), (codes[...] & 127, lane)):
            found = dot(got.astype(f32), hot, (1, 0))
            where[pl.ds(i, 1), :] = jnp.sum(jnp.where(at, found, 0.0), axis=0, keepdims=True).astype(i32)
        return carry

    lax.fori_loop(0, ITEMS // 4, place, 0, unroll=5)
    for i in range(ITEMS // 8):
        tops[i : i + 1, :] = jnp.concatenate([wanted[8 * i + u : 8 * i + u + 1, 64:96] for u in range(8)], axis=1)
    for c in to_scalars:
        c.wait()
    number = row_iota((SUB, 128)) * 128 + lax.broadcasted_iota(i32, (SUB, 128), 1)

    def find(w, found):
        for k in range(SUB):
            found = jnp.where(number == work_s[k, 4, w], k * 64 + w, found)
        return found

    slots[...] = lax.fori_loop(0, ITEMS, find, jnp.full((SUB, 128), -1, i32), unroll=4)
    slot_copy = pltpu.make_async_copy(slots, slot_s, local_sem.at[9])
    slot_copy.start()

    done(flight)
    top_sums(table_1, part_1)
    flight = send(part_1.at[g], across)
    x_3 = ring_3(x, x_1, x_2)
    essential_cells(table_1)
    done(flight)
    four_parts(top_1, part_1)
    flight = send(top_1.at[s], within)
    done(x_3)
    ahead_1 = ring_1(ahead)
    slot_copy.wait()

    def load_1(n):
        return x[(n >> 7) & 1, n >> 8, n & 127]

    near_part(load_1, 0, 8)
    done(flight)
    top_cells(top_1)
    ahead_2 = finish(load_1, force_1, 8, lambda: ring_2(ahead, ahead_1))

    def second(b, carry):
        sl = pl.ds(pl.multiple_of(b * WIDE, WIDE), WIDE)
        push = kick * act[:, sl].astype(f32) * forced(force_1, slot_s[s, b])
        h = half[:, sl] + push + push
        p = x[core, chip, b][0:3] + time_step * h
        half[:, sl] = h
        pos_out[:, sl] = p
        for c in range(3):
            dense[c, pl.ds(b, 1), :] = p[c : c + 1]
        return carry

    lax.fori_loop(0, BUCKETS, second, 0, unroll=4)
    moments(dense, top_row[...].astype(f32), table_2.at[core, chip, g])
    flight = send(table_2.at[core, chip, g], along)
    ahead_3 = ring_3(ahead, ahead_1, ahead_2)
    done(flight)
    flight = send(table_2.at[core, :, g], across)
    done(ahead_3)

    def load_2(n):
        at = ((n >> 7) & 1, n >> 8, n & 127)
        p = ahead[at]
        moved = p[0:3] + (2.0 * kick * time_step) * p[3:4] * forced(force_1, slot_s[n >> 7, n & 127])
        return jnp.concatenate([moved, x[at][3:4]], axis=0)

    near_part(load_2, 0, 12)
    done(flight)
    flight = send(table_2.at[core], [sibling])
    near_part(load_2, 12, 20)
    done(flight)
    top_sums(table_2, part_2)
    flight = send(part_2.at[g], across)
    essential_cells(table_2)
    done(flight)
    four_parts(top_2, part_2)
    flight = send(top_2.at[s], within)
    near_part(load_2, 20, 24)
    done(flight)
    top_cells(top_2)
    finish(load_2, force_2, 24)

    def last(b, carry):
        sl = pl.ds(pl.multiple_of(b * WIDE, WIDE), WIDE)
        vel_out[:, sl] = half[:, sl] + kick * act[:, sl].astype(f32) * forced(force_2, slot_s[s, b])
        return carry

    lax.fori_loop(0, BUCKETS, last, 0, unroll=4)


def body(positions, velocities, masses, accel_prev, active, bucket_top, near_list, cell_list, top_list, essential, work):
    n = positions.shape[1]
    vm, dma = pltpu.VMEM, pltpu.SemaphoreType.DMA
    flat = vm((3, n), f32)
    group = vm((2, SUB // 2, BUCKETS, 4, WIDE), f32)
    twice = [
        vm((2, SUB // 2, DOM, 16, 128), f32), vm((SUB, 4, 16, 128), f32), vm((DOM, 16, 128), f32),
        vm((2, SUB // 2, 3, ITEMS, WIDE), f32),
    ]
    scratch = [flat, flat, flat, vm((1, n), i32), vm((1, n), f32), flat, vm((4, BUCKETS, WIDE), f32), group, group]
    scratch += twice + twice
    scratch += [
        vm((48, 32), f32), vm((SUB * DOM * 16, 256), bf16), vm((32 * 16, 256), bf16),
        vm((ITEMS, 16, 128), f32), vm((ITEMS, 4, WIDE), f32),
        vm((2, SUB // 2, BUCKETS + 8, 128), i32), vm((ITEMS, 128), i32), vm((32, 128), i32),
        vm((16, 256), i32), vm((16, 256), i32), vm((8, 256), i32), vm((SUB, 128), i32),
        pltpu.SMEM((ITEMS, 128), i32), pltpu.SMEM((SUB, 8, 128), i32), pltpu.SMEM((SUB, 128), i32),
        dma((5,)), dma((COPIES,)), dma((COPIES,)), dma((10,)),
    ]
    place = lambda where: pl.BlockSpec(memory_space=where)
    shape = jax.ShapeDtypeStruct((3, n), f32)
    return pl.pallas_call(
        kernel,
        out_shape=(shape, shape),
        in_specs=[place(pltpu.SMEM)] + [place(pltpu.HBM)] * 5 + [place(pltpu.VMEM)] * 6,
        out_specs=(place(pltpu.VMEM), place(pltpu.VMEM)),
        scratch_shapes=scratch,
        compiler_params=pltpu.CompilerParams(collective_id=1, has_side_effects=True, vmem_limit_bytes=62 * MIB),
    )(
        work, positions, velocities, accel_prev, active.reshape(1, n), masses.reshape(1, n),
        bucket_top.reshape(1, BUCKETS), cell_list.T, top_list.T, near_list.T, essential.reshape(DOM, -1),
        work.reshape(1, ITEMS),
    )


def solution(mesh):
    both = ("dom", "sub")
    in_specs = (
        P(None, both), P(None, both), P(both), P(None, both), P(both), P(both),
        P(both, None), P(both, None), P(both, None), P("dom", "sub", None, None), P(both),
    )
    return jax.shard_map(
        body, mesh=mesh, in_specs=in_specs, out_specs=(P(None, both), P(None, both)), check_vma=False
    )
```

```python
import functools

import jax
import jax.numpy as jnp
from jax import lax
from jax.experimental import pallas as pl
from jax.experimental.pallas import tpu as pltpu
from jax.sharding import PartitionSpec as P

f32, bf16, i32 = jnp.float32, jnp.bfloat16, jnp.int32
MESH = pl.DeviceIdType.MESH
SUB, DOM = 8, 16
BUCKETS, WIDE, ITEMS = 128, 256, 40
GROUP = SUB * BUCKETS
TOP_SIDE = 16
MIB = 2**20

time_step = 0.01
soften = 0.0025
mass_floor = 0.5
kick = 0.5 * time_step
PAIRS = ((0, 0), (1, 1), (2, 2), (0, 1), (0, 2), (1, 2))
NEAR_AT = 96
COPIES = 160


def rnd(a):
    return a.astype(bf16).astype(f32)


def split3(a):
    h = rnd(a)
    r = a - h
    m = rnd(r)
    return h, m, rnd(r - m)


def dot(a, b, dims):
    return lax.dot_general(
        a.astype(bf16), b.astype(bf16), ((dims[:1], dims[1:]), ((), ())), preferred_element_type=f32
    )


def row_iota(shape):
    return lax.broadcasted_iota(i32, shape, 0)


def pick(rows, shape):
    at = row_iota(shape)
    out = jnp.zeros(shape, f32)
    for i, v in rows.items():
        out = jnp.where(at == i, v, out)
    return out


def square(y):
    q = y * y
    return q[0:1] + q[1:2] + q[2:3]


def moments(dense, top_row, rec_ref):
    first = [dense[c][:, 0:1] for c in range(3)]
    y = [dense[c] - first[c] for c in range(3)]
    m = dense[3]
    ones = jnp.ones((16, WIDE), f32)
    lead = jnp.where(lax.broadcasted_iota(i32, (16, WIDE), 1) == 0, 1.0, 0.0)

    def total(a, by=ones):
        h, m, l = split3(a)
        return (dot(by, h, (1, 1)) + (dot(by, m, (1, 1)) + dot(by, l, (1, 1))))[0:1]

    my = [m * y[c] for c in range(3)]
    mass = total(m)
    start = [total(dense[c], lead) for c in range(3)]
    s = [total(my[c]) for c in range(3)]
    d = [s[c] / mass for c in range(3)]
    second = [total(my[a] * y[b]) - s[a] * d[b] for a, b in PAIRS]
    rows = {0: mass, 10: top_row}
    for c in range(3):
        rows[1 + c] = start[c] + d[c]
    for k in range(6):
        rows[4 + k] = second[k]
    rec_ref[...] = pick(rows, (16, BUCKETS))


def centre(ids):
    return [
        (part.astype(f32) + 0.5) / TOP_SIDE
        for part in (ids >> 8, (ids >> 4) & 15, ids & 15)
    ]


def spread(table, pieces, rows):
    at = row_iota((16, 128))
    extra = (at >= 11) & (at < 14)

    def step(k, carry):
        t = table(k)
        h, m, l = split3(t)
        low = pltpu.roll(l, 10, 0)
        both = jnp.concatenate([jnp.where(extra, low, h), jnp.where(extra, 0.0, m)], axis=1)
        pieces[pl.ds(pl.multiple_of(k * 16, 16), 16), :] = both.astype(bf16)
        return carry

    lax.fori_loop(0, rows, step, 0, unroll=4)


def lookup(pieces, rows, row, lane):
    n = row.shape[1]
    hot = jnp.where(row_iota((128, n)) == lane, 1.0, 0.0).astype(bf16)
    hot = jnp.concatenate([hot, hot], axis=0)
    row16 = jnp.broadcast_to(row, (16, n))

    def step(i, got):
        block = pieces[pl.ds(pl.multiple_of(i * 128, 128), 128), :]
        found = dot(block, hot, (1, 0))
        for u in range(8):
            got = jnp.where(row16 == i * 8 + u, found[u * 16 : u * 16 + 16], got)
        return got

    return lax.fori_loop(0, rows // 8, step, jnp.zeros((16, n), f32), unroll=rows // 8)


def from_first(first):
    is_pos = row_iota((4, WIDE)) < 3
    origin = jnp.where(is_pos, jnp.broadcast_to(first[:, 0:1], (4, WIDE)), 0.0)
    return is_pos, origin, first - origin


def near_item(load, ids):
    first = load(ids[0])
    is_pos, origin, y = from_first(first)
    h = rnd(y)
    mid = rnd(y - h)
    fine = h + mid
    th, tm, tl = split3(square(fine))
    far_h = jnp.where(is_pos, -2.0 * h, 0.0)
    far_m = jnp.where(is_pos, -2.0 * mid, 0.0)
    one = jnp.ones((1, WIDE), f32)
    ct = pick({0: one, 1: one, 2: one, 3: th, 4: tm, 5: tl}, (8, WIDE))
    target = jnp.concatenate([far_h, far_h, far_m, far_m, ct], axis=0).astype(bf16)
    total = jnp.zeros((WIDE, 16), f32)
    for k in range(4):
        raw = first if k == 0 else load(ids[k])
        ys = raw - origin
        sh = rnd(ys)
        sm = rnd(ys - sh)
        sf = sh + sm
        qh, qm, ql = split3(square(sf) + soften)
        cs = pick({0: qh, 1: qm, 2: ql, 3: one, 4: one, 5: one}, (8, WIDE))
        source = jnp.concatenate([sh, sm, sh, sm, cs], axis=0)
        r = lax.rsqrt(dot(target, source, (0, 0)))
        w = (r * r * r).astype(bf16)
        z = jnp.where(is_pos, sf * raw[3:4], raw)
        zh, zm, zl = split3(z)
        left = jnp.concatenate([zh, zm, zl, jnp.zeros((4, WIDE), f32)], axis=0)
        total = total + dot(w, left, (1, 1))
    total = total.T
    s = total[0:4] + total[4:8] + total[8:12]
    return s - fine * s[3:4]


def far_item(cells, origin, y):
    o = [jnp.broadcast_to(origin[i : i + 1, 0:1], (1, 128)) for i in range(3)]
    mass = cells[0:1]
    px, py, pz = [cells[1 + c : 2 + c] + cells[11 + c : 12 + c] - o[c] for c in range(3)]
    trace = cells[4:5] + cells[5:6] + cells[6:7]
    qxx, qyy, qzz = [3.0 * cells[i : i + 1] - trace for i in (4, 5, 6)]
    qxy, qxz, qyz = [3.0 * cells[i : i + 1] for i in (7, 8, 9)]
    gx = qxx * px + qxy * py + qxz * pz
    gy = qxy * px + qyy * py + qyz * pz
    gz = qxz * px + qyz * py + qzz * pz
    one = jnp.ones((1, 128), f32)
    pp = px * px + py * py + pz * pz + soften
    cs = pick({0: pp, 1: -2.0 * px, 2: -2.0 * py, 3: -2.0 * pz, 4: one, 5: one, 6: one}, (16, 128))
    pg = px * gx + py * gy + pz * gz
    cq = pick(
        {0: pg, 1: -2.0 * gx, 2: -2.0 * gy, 3: -2.0 * gz, 4: qxx, 5: qyy, 6: qzz, 7: 2.0 * qxy, 8: 2.0 * qxz, 9: 2.0 * qyz},
        (16, 128),
    )
    c = jnp.concatenate([cs, cq], axis=1)
    a, b, d = y[0:1], y[1:2], y[2:3]
    ones = jnp.ones((1, WIDE), f32)
    phi = pick(
        {0: ones, 1: a, 2: b, 3: d, 4: a * a, 5: b * b, 6: d * d, 7: a * b, 8: a * d, 9: b * d}, (16, WIDE)
    )
    ch, cm, cl = split3(c)
    fh, fm, fl = split3(phi)
    sq = dot(
        jnp.concatenate([fh, fm, fh, fm, fl, fh], axis=0),
        jnp.concatenate([ch, ch, cm, cm, ch, cl], axis=0),
        (0, 0),
    )
    s, q = sq[:, 0:128], sq[:, 128:256]
    r = lax.rsqrt(s)
    r2 = r * r
    r3 = r * r2
    r5 = r3 * r2
    l1 = pick({0: mass * px, 1: mass * py, 2: mass * pz, 3: -mass}, (16, 128))
    l2 = pick({0: 2.5 * px, 1: 2.5 * py, 2: 2.5 * pz, 3: -2.5 * one}, (16, 128))
    l3 = pick({0: -gx, 1: -gy, 2: -gz, 4: qxx, 5: qyy, 6: qzz, 7: qxy, 8: qxz, 9: qyz}, (16, 128))
    out = jnp.zeros((WIDE, 32), f32)
    for l, v in ((l1, r3), (l2, q * (r5 * r2)), (l3, r5)):
        lh = rnd(l)
        pieces = jnp.concatenate([lh, rnd(l - lh)], axis=0)
        vh = v.astype(bf16)
        vm = (v - vh.astype(f32)).astype(bf16)
        out = out + dot(
            jnp.concatenate([vh, vm], axis=1), jnp.concatenate([pieces, pieces], axis=1), (1, 1)
        )
    out = out.T
    t = out[0:16] + out[16:32]
    axx, ayy, azz, axy, axz, ayz = [t[i : i + 1] for i in range(4, 10)]
    turned = pick(
        {0: axx * a + axy * b + axz * d, 1: axy * a + ayy * b + ayz * d, 2: axz * a + ayz * b + azz * d}, (4, WIDE)
    )
    return t[0:4] + t[3:4] * y + turned


def top_values(t, ids):
    mass = t[0:1]
    own = t[10:11].astype(i32)
    d = [t[1 + c : 2 + c] - at for c, at in enumerate(centre(own))]
    md = [mass * d[c] for c in range(3)]
    rows = {0: mass, 1: md[0], 2: md[1], 3: md[2]}
    for k, (a, b) in enumerate(PAIRS):
        rows[4 + k] = t[4 + k : 5 + k] + md[a] * d[b]
    pieces = jnp.concatenate(split3(pick(rows, (16, BUCKETS))), axis=0)
    return pieces, jnp.where(ids == own, 1.0, 0.0)


def top_record(t, base):
    mass = t[0:1]
    w = jnp.maximum(mass, mass_floor)
    at = centre(lax.broadcasted_iota(i32, (1, 32), 1) + base)
    u = [t[1 + c : 2 + c] / w for c in range(3)]
    rows = {0: mass}
    for c in range(3):
        rows[1 + c] = at[c] + u[c]
    for k, (a, b) in enumerate(PAIRS):
        rows[4 + k] = t[4 + k : 5 + k] - t[1 + a : 2 + a] * u[b]
    return pick(rows, (16, 32))


def by_core(s):
    return (s & 1) * (SUB // 2) + (s >> 1)


def forced(force, slot):
    k = jnp.maximum(slot, 0)
    rows = [force[k >> 8, (k >> 6) & 3, c, pl.ds(k & 63, 1), :] for c in range(3)]
    return jnp.where(slot >= 0, jnp.concatenate(rows, axis=0), 0.0)


def kernel(
    work, pos_in, vel_in, acc_in, act_in, mass_in, top_row, cell_list, top_list, near_list, requests, work_row,
    vel_out, pos_out,
    pos, vel, acc, act, mass, half, dense, x, ahead,
    table_1, top_1, part_1, force_1, table_2, top_2, part_2, force_2,
    sums, pieces, top_pieces, cells, pairs,
    lists, wanted, codes, row, lane, tops, slots, near_s, work_s, slot_s,
    load_sem, send_sem, recv_sem, local_sem,
):
    g, s = lax.axis_index("dom"), lax.axis_index("sub")
    core, chip = lax.rem(s, 2), s // 2
    sibling = (g, s + 1 - 2 * core)
    up, down, over = [(g, lax.rem(s + k, SUB)) for k in (2, 6, 4)]
    along = [up, down, over]
    across = [(lax.rem(g + k, DOM), s) for k in range(1, DOM)]
    within = [(g, lax.rem(s + k, SUB)) for k in range(1, SUB)]
    used = [0]

    inputs = [
        pltpu.make_async_copy(a, b, load_sem.at[k])
        for k, (a, b) in enumerate(((pos_in, pos), (vel_in, vel), (acc_in, acc), (act_in, act), (mass_in, mass)))
    ]
    for c in inputs:
        c.start()

    barrier = pltpu.get_barrier_semaphore()
    for peer in across + within:
        pl.semaphore_signal(barrier, inc=1, device_id=peer, device_id_type=MESH)
    def send(ref, peers, source=None):
        copies = []
        for peer in peers:
            k = used[0]
            used[0] += 1
            copies.append(
                pltpu.make_async_remote_copy(
                    src_ref=ref if source is None else source, dst_ref=ref, send_sem=send_sem.at[k],
                    recv_sem=recv_sem.at[k], device_id=peer, device_id_type=MESH,
                )
            )
            copies[-1].start()
        return copies

    def done(copies):
        for c in copies:
            c.wait()

    below, above, facing = [lax.rem(chip + k, 4) for k in (3, 1, 2)]
    low, high = pl.ds(0, BUCKETS // 2), pl.ds(BUCKETS // 2, BUCKETS // 2)

    def ring_1(buf):
        return send(buf.at[core, chip], [up, down, sibling])

    def ring_2(buf, first):
        first[0].wait_recv()
        found = send(buf.at[core, below, low], [up])
        more = send(buf.at[core, below], [sibling])
        first[1].wait_recv()
        found += send(buf.at[core, above, high], [down])
        more += send(buf.at[core, above], [sibling])
        return found, more

    def ring_3(buf, first, second):
        found, more = second
        for c in found:
            c.wait_recv()
        final = send(buf.at[core, facing], [sibling])
        for c in first + found:
            c.wait_send()
        first[2].wait_recv()
        done(more)
        return final

    for c in inputs:
        c.wait()

    def first(b, carry):
        sl = pl.ds(pl.multiple_of(b * WIDE, WIDE), WIDE)
        a = act[:, sl].astype(f32)
        h = vel[:, sl] + kick * a * acc[:, sl]
        p = pos[:, sl] + time_step * h
        half[:, sl] = h
        x[core, chip, b] = jnp.concatenate([p, mass[:, sl]], axis=0)
        return carry

    lax.fori_loop(0, BUCKETS, first, 0, unroll=8)
    pl.semaphore_wait(barrier, DOM + SUB - 2)
    x_1 = ring_1(x)

    def onward(b, carry):
        sl = pl.ds(pl.multiple_of(b * WIDE, WIDE), WIDE)
        p = x[core, chip, b]
        next_p = p[0:3] + time_step * half[:, sl]
        ahead[core, chip, b] = jnp.concatenate([next_p, act[:, sl].astype(f32)], axis=0)
        for c in range(4):
            dense[c, pl.ds(b, 1), :] = p[c : c + 1]
        return carry

    lax.fori_loop(0, BUCKETS, onward, 0, unroll=8)
    turned = [cell_list[...], top_list[...], near_list[...], jnp.zeros((28, BUCKETS), i32)]
    lists[core, chip, 0:BUCKETS, :] = jnp.concatenate(turned, axis=0).T
    asked = requests[...]
    asked = (by_core(asked >> 7) * DOM + row_iota((DOM, 32))) * 128 + (asked & 127)
    rest = [jnp.concatenate([asked[4 * r + k : 4 * r + k + 1] for k in range(4)], axis=1) for r in range(4)]
    rest.append(jnp.concatenate([work_row[...], jnp.full((1, 128 - ITEMS), -1, i32)], axis=1))
    lists[core, chip, BUCKETS : BUCKETS + 8, :] = jnp.concatenate(rest + [jnp.zeros((3, 128), i32)], axis=0)
    list_copies = send(lists.at[core, chip], along)

    def near_part(load, begin, end):
        def item(w, carry):
            pairs[w] = near_item(load, [near_s[w, NEAR_AT + k] for k in range(4)])
            return carry

        lax.fori_loop(begin, end, item, 0, unroll=4)

    def top_sums(table, part):
        base = (s * DOM + g) * 32
        ids = lax.broadcasted_iota(i32, (32, BUCKETS), 0) + base
        sums[...] = jnp.zeros_like(sums)

        def step(i, carry):
            at, k = i >> 2, (i & 3) * 4
            got = [top_values(table[at >> 2, at & 3, k + u], ids) for u in range(4)]
            v = jnp.concatenate([a for a, _ in got], axis=1)
            o = jnp.concatenate([b for _, b in got], axis=1)
            sums[...] += dot(v, o, (1, 1))
            return carry

        lax.fori_loop(0, SUB * DOM // 4, step, 0, unroll=4)
        mine = top_record(sums[0:16] + sums[16:32] + sums[32:48], base)
        four = jnp.concatenate([mine] * 4, axis=1)
        quarter = lax.broadcasted_iota(i32, (16, 128), 1) // 32
        part[g] = jnp.where(quarter == lax.rem(g, 4), four, 0.0)

    def four_parts(top, part):
        for k in range(4):
            top[s, k] = part[4 * k] + part[4 * k + 1] + part[4 * k + 2] + part[4 * k + 3]

    def essential_cells(table):
        spread(lambda k: table[k >> 6, (k >> 4) & 3, k & 15], pieces, SUB * DOM)

        def gather(i, carry):
            ess = lookup(pieces, SUB * DOM, row[pl.ds(i, 1), :], lane[pl.ds(i, 1), :])
            blank = jnp.zeros((16, 64), f32)
            for u in range(4):
                cells[i * 4 + u] = jnp.concatenate([ess[:, u * 64 : u * 64 + 64], blank], axis=1)
            return carry

        lax.fori_loop(0, ITEMS // 4, gather, 0, unroll=2)

    def top_cells(top):
        spread(lambda k: top[k >> 2, k & 3], top_pieces, 32)

        def gather(i, carry):
            t = tops[pl.ds(i, 1), :]
            far = lookup(top_pieces, 32, t >> 7, t & 127)
            blank = [jnp.zeros((16, n), f32) for n in (64, 32)]
            for u in range(8):
                cells[i * 8 + u] += jnp.concatenate([blank[0], far[:, u * 32 : u * 32 + 32], blank[1]], axis=1)
            return carry

        lax.fori_loop(0, ITEMS // 8, gather, 0, unroll=5)

    def finish(load, force, known, between=None):
        first_sem = used[0]
        used[0] += 16

        def copy(ref, k, peer):
            return pltpu.make_async_remote_copy(
                src_ref=ref, dst_ref=ref, send_sem=send_sem.at[k], recv_sem=recv_sem.at[k],
                device_id=peer, device_id_type=MESH,
            )

        def rows(p):
            return pl.ds(pl.multiple_of(p * 8, 8), 8)

        def by_links(p):
            ref = force.at[core, chip, :, rows(p), :]
            return [copy(ref, first_sem + p * 3 + k, peer) for k, peer in enumerate(along)]

        def to_sibling(p):
            return copy(force.at[core, :, :, rows(p), :], first_sem + 12 + p, sibling)

        def forward(p):
            done(by_links(p))
            to_sibling(p).start()

        def compute(p, with_near):
            def item(i, carry):
                w = p * 8 + i
                _, origin, y = from_first(load(near_s[w, NEAR_AT]))
                if with_near:
                    a = near_item(load, [near_s[w, NEAR_AT + k] for k in range(4)])
                else:
                    a = pairs[w]
                a = a + far_item(cells[w], origin, y)
                for c in range(3):
                    force[core, chip, c, pl.ds(w, 1), :] = a[c : c + 1]
                return carry

            lax.fori_loop(0, 8, item, 0, unroll=4)

        def piece(p, carry, with_near):
            compute(p, with_near)
            for c in by_links(p):
                c.start()

            return carry

        if known:
            lax.fori_loop(0, known // 8, functools.partial(piece, with_near=False), 0)
        if known < 24:
            lax.fori_loop(known // 8, 3, functools.partial(piece, with_near=True), 0)
        middle = between() if between else None
        lax.fori_loop(3, 4, functools.partial(piece, with_near=True), 0)
        compute(4, True)
        final = send(force.at[core, chip, :, pl.ds(32, 8), :], within)
        for p in range(4):
            forward(p)
        done(final)
        for p in range(4):
            to_sibling(p).wait()
        return middle

    moments(dense, top_row[...].astype(f32), table_1.at[core, chip, g])
    flight = send(table_1.at[core, chip, g], along)
    done(flight)
    flight = send(table_1.at[core, :, g], across)
    done(list_copies)
    list_copies = send(lists.at[core], [sibling])
    x_2 = ring_2(x, x_1)
    done(flight)
    flight = send(table_1.at[core], [sibling])
    done(list_copies)

    def take(w, carry):
        n = work[w]
        wanted[pl.ds(w, 1), :] = lists[(n >> 7) & 1, n >> 8, pl.ds(n & 127, 1), :]
        return carry

    lax.fori_loop(0, ITEMS, take, 0, unroll=4)
    to_scalars = [pltpu.make_async_copy(wanted, near_s, local_sem.at[0])]
    for k in range(SUB):
        to_scalars.append(
            pltpu.make_async_copy(lists.at[k // 4, k % 4, pl.ds(128, 8)], work_s.at[k], local_sem.at[1 + k])
        )
    for c in to_scalars:
        c.start()
    for k in range(SUB):
        codes[4 * k : 4 * k + 4, :] = lists[k % 2, k // 2, 128:132, :]

    def place(i, carry):
        ids = jnp.concatenate([wanted[pl.ds(4 * i + u, 1), :][:, 0:64] for u in range(4)], axis=1)
        hot = jnp.where(row_iota((128, 256)) == (ids & 127), 1.0, 0.0)
        at = row_iota((32, 256)) == (ids >> 7)
        for got, where in ((codes[...] >> 7, row), (codes[...] & 127, lane)):
            found = dot(got.astype(f32), hot, (1, 0))
            where[pl.ds(i, 1), :] = jnp.sum(jnp.where(at, found, 0.0), axis=0, keepdims=True).astype(i32)
        return carry

    lax.fori_loop(0, ITEMS // 4, place, 0, unroll=5)
    for i in range(ITEMS // 8):
        tops[i : i + 1, :] = jnp.concatenate([wanted[8 * i + u : 8 * i + u + 1, 64:96] for u in range(8)], axis=1)
    for c in to_scalars:
        c.wait()
    number = row_iota((SUB, 128)) * 128 + lax.broadcasted_iota(i32, (SUB, 128), 1)

    def find(w, found):
        for k in range(SUB):
            found = jnp.where(number == work_s[k, 4, w], k * 64 + w, found)
        return found

    slots[...] = lax.fori_loop(0, ITEMS, find, jnp.full((SUB, 128), -1, i32), unroll=4)
    slot_copy = pltpu.make_async_copy(slots, slot_s, local_sem.at[9])
    slot_copy.start()

    done(flight)
    top_sums(table_1, part_1)
    flight = send(part_1.at[g], across)
    x_3 = ring_3(x, x_1, x_2)
    essential_cells(table_1)
    done(flight)
    four_parts(top_1, part_1)
    flight = send(top_1.at[s], within)
    done(x_3)
    ahead_1 = ring_1(ahead)
    slot_copy.wait()

    def load_1(n):
        return x[(n >> 7) & 1, n >> 8, n & 127]

    near_part(load_1, 0, 8)
    done(flight)
    top_cells(top_1)
    ahead_2 = finish(load_1, force_1, 8, lambda: ring_2(ahead, ahead_1))

    def second(b, carry):
        sl = pl.ds(pl.multiple_of(b * WIDE, WIDE), WIDE)
        push = kick * act[:, sl].astype(f32) * forced(force_1, slot_s[s, b])
        h = half[:, sl] + push + push
        p = x[core, chip, b][0:3] + time_step * h
        half[:, sl] = h
        pos_out[:, sl] = p
        for c in range(3):
            dense[c, pl.ds(b, 1), :] = p[c : c + 1]
        return carry

    lax.fori_loop(0, BUCKETS, second, 0, unroll=4)
    moments(dense, top_row[...].astype(f32), table_2.at[core, chip, g])
    flight = send(table_2.at[core, chip, g], along)
    ahead_3 = ring_3(ahead, ahead_1, ahead_2)
    done(flight)
    flight = send(table_2.at[core, :, g], across)
    done(ahead_3)

    def load_2(n):
        at = ((n >> 7) & 1, n >> 8, n & 127)
        p = ahead[at]
        moved = p[0:3] + (2.0 * kick * time_step) * p[3:4] * forced(force_1, slot_s[n >> 7, n & 127])
        return jnp.concatenate([moved, x[at][3:4]], axis=0)

    near_part(load_2, 0, 12)
    done(flight)
    flight = send(table_2.at[core], [sibling])
    near_part(load_2, 12, 20)
    done(flight)
    top_sums(table_2, part_2)
    flight = send(part_2.at[g], across)
    essential_cells(table_2)
    done(flight)
    four_parts(top_2, part_2)
    flight = send(top_2.at[s], within)
    near_part(load_2, 20, 24)
    done(flight)
    top_cells(top_2)
    finish(load_2, force_2, 24)

    def last(b, carry):
        sl = pl.ds(pl.multiple_of(b * WIDE, WIDE), WIDE)
        vel_out[:, sl] = half[:, sl] + kick * act[:, sl].astype(f32) * forced(force_2, slot_s[s, b])
        return carry

    lax.fori_loop(0, BUCKETS, last, 0, unroll=4)


def body(positions, velocities, masses, accel_prev, active, bucket_top, near_list, cell_list, top_list, essential, work):
    n = positions.shape[1]
    vm, dma = pltpu.VMEM, pltpu.SemaphoreType.DMA
    flat = vm((3, n), f32)
    group = vm((2, SUB // 2, BUCKETS, 4, WIDE), f32)
    twice = [
        vm((2, SUB // 2, DOM, 16, 128), f32), vm((SUB, 4, 16, 128), f32), vm((DOM, 16, 128), f32),
        vm((2, SUB // 2, 3, ITEMS, WIDE), f32),
    ]
    scratch = [flat, flat, flat, vm((1, n), i32), vm((1, n), f32), flat, vm((4, BUCKETS, WIDE), f32), group, group]
    scratch += twice + twice
    scratch += [
        vm((48, 32), f32), vm((SUB * DOM * 16, 256), bf16), vm((32 * 16, 256), bf16),
        vm((ITEMS, 16, 128), f32), vm((ITEMS, 4, WIDE), f32),
        vm((2, SUB // 2, BUCKETS + 8, 128), i32), vm((ITEMS, 128), i32), vm((32, 128), i32),
        vm((16, 256), i32), vm((16, 256), i32), vm((8, 256), i32), vm((SUB, 128), i32),
        pltpu.SMEM((ITEMS, 128), i32), pltpu.SMEM((SUB, 8, 128), i32), pltpu.SMEM((SUB, 128), i32),
        dma((5,)), dma((COPIES,)), dma((COPIES,)), dma((10,)),
    ]
    place = lambda where: pl.BlockSpec(memory_space=where)
    shape = jax.ShapeDtypeStruct((3, n), f32)
    return pl.pallas_call(
        kernel,
        out_shape=(shape, shape),
        in_specs=[place(pltpu.SMEM)] + [place(pltpu.HBM)] * 5 + [place(pltpu.VMEM)] * 6,
        out_specs=(place(pltpu.VMEM), place(pltpu.VMEM)),
        scratch_shapes=scratch,
        compiler_params=pltpu.CompilerParams(collective_id=1, has_side_effects=True, vmem_limit_bytes=62 * MIB),
    )(
        work, positions, velocities, accel_prev, active.reshape(1, n), masses.reshape(1, n),
        bucket_top.reshape(1, BUCKETS), cell_list.T, top_list.T, near_list.T, essential.reshape(DOM, -1),
        work.reshape(1, ITEMS),
    )


def solution(mesh):
    both = ("dom", "sub")
    in_specs = (
        P(None, both), P(None, both), P(both), P(None, both), P(both), P(both),
        P(both, None), P(both, None), P(both, None), P("dom", "sub", None, None), P(both),
    )
    return jax.shard_map(
        body, mesh=mesh, in_specs=in_specs, out_specs=(P(None, both), P(None, both)), check_vma=False
    )
```
